256 devices in a mesh: ka: 8 (over x, y_hi), sa: 32 (over y_lo, z, core).
Axes of the slice: x: 4, y: 4 (y_hi: 2, y_lo: 2; y = y_hi * 2 + y_lo), z: 8, core: 2. Of those that a mesh axis runs over, the one named last changes fastest.
Arguments:
- wave_in: float32 [8, 2, 384, 18432], P('ka', None, 'sa'), may hold values from -6 to 6
- potential: float32 [384, 18432], P('sa'), may hold values from -3.140625 to 3.140625
- absorb_radial: float32 [384], P('sa'), may hold values from 0 to 0.6
- absorb_bond: float32 [192], replicated, may hold values from 0 to 0.6
- coriolis_weight: float32 [384], P('sa'), may hold values from 0.002 to 0.03
- ladder: float32 [96, 96], replicated, may hold values from -0.625 to 0.625
- angle_step: float32 [8, 2, 96, 96], P('ka'), may hold values from -0.3125 to 0.3125
- bond_step: float32 [2, 192, 192], replicated, may hold values from -0.21875 to 0.21875
- radial_step: float32 [2, 384, 384], replicated, may hold values from -0.15625 to 0.15625
Outputs:
- wave_out: float32 [8, 2, 384, 18432], P('ka', None, 'sa')
The draws below stay inside these ranges and needn't reach their ends.
All inputs are finite; a program needn't handle non-finite values.
Results may differ from the reference program's by a relative error of at most 0.00007.
Values sent between devices are 32-bit elements; how exact they have to be, the bound alone decides.
A program may use at most 64 MiB of HBM per device.

```python
import math
import jax
import jax.numpy as jnp
from jax import lax

R = 384
RR = 192
TH = 96
KTOT = 8
RT = 18432


def steps_of(rng, shape, shards, smallest, largest):
    level, own = 1.0, jax.random.fold_in(rng, 6)
    for axis_at, parts in shards:
        draws = jnp.exp(jax.random.uniform(jax.random.fold_in(own, axis_at), (parts,), jnp.float32, smallest / len(shards), largest / len(shards)))
        level = level * jnp.repeat(draws, shape[axis_at] // parts).reshape([-1 if axis == axis_at else 1 for axis in range(len(shape))])
    return level


def scatter_about(rng, extent, deviation, most, cuts=(), held_as=jnp.bfloat16):
    factor_of = steps_of(rng, extent, cuts, -0.22, 0.18) if cuts else 1.0
    drawn = jax.random.normal(rng, extent, jnp.float32) * deviation * factor_of
    return jnp.minimum(jnp.maximum(drawn, -most), most).astype(held_as)


def setup_inputs(seed: int = 0) -> dict:
    splits = jax.random.split(jax.random.key(seed), 10)
    return {
        "wave_in": scatter_about(splits[0], (KTOT, 2, R, RT), 1.0, 6.0, ((0, 8), (2, 32)), jnp.float32),
        "potential": jnp.clip(jax.random.uniform(splits[1], (R, RT), jnp.float32, -3.140625, 3.140625), -3.140625, 3.140625),
        "absorb_radial": jnp.clip(0.6 * jax.random.uniform(splits[2], (R,), jnp.float32) ** steps_of(splits[2], (R,), ((0, 32),), -0.2, 0.2), 0.0, 0.6),
        "absorb_bond": jnp.clip(jax.random.uniform(splits[3], (RR,), jnp.float32, 0.0, 0.6), 0.0, 0.6),
        "coriolis_weight": jnp.clip(jnp.exp(math.log(0.03) - 2.70805 * jax.random.uniform(splits[4], (R,), jnp.float32) ** steps_of(splits[4], (R,), ((0, 32),), -0.2, 0.2)), 0.002, 0.03),
        "ladder": scatter_about(splits[5], (TH, TH), TH ** -0.5, 0.625, (), jnp.float32),
        "angle_step": scatter_about(splits[6], (KTOT, 2, TH, TH), (4 * TH) ** -0.5, 0.3125, ((0, 8),), jnp.float32),
        "bond_step": scatter_about(splits[7], (2, RR, RR), (4 * RR) ** -0.5, 0.21875, (), jnp.float32),
        "radial_step": scatter_about(splits[8], (2, R, R), (4 * R) ** -0.5, 0.15625, (), jnp.float32),
    }


def product(form, left_side, right_side):
    return jnp.einsum(form, left_side, right_side, precision=lax.Precision.HIGHEST)

def complex_apply(form, operator_real, operator_imag, real_part, imag_part):
    new_real = product(form, operator_real, real_part) - product(form, operator_imag, imag_part)
    new_imag = product(form, operator_real, imag_part) + product(form, operator_imag, real_part)
    return (new_real, new_imag)

def complex_scale(scale_real, scale_imag, real_part, imag_part):
    return (scale_real * real_part - scale_imag * imag_part, scale_real * imag_part + scale_imag * real_part)

def reference(wave_in, potential, absorb_radial, absorb_bond, coriolis_weight, ladder, angle_step, bond_step, radial_step):
    wave = wave_in.reshape(KTOT, 2, R, RR, TH)
    damping = jnp.exp(-0.5 * (absorb_radial[:, None, None] + absorb_bond[None, :, None]))
    phase_angle = 0.5 * potential.reshape(R, RR, TH)
    factor_real = damping * jnp.cos(phase_angle)
    factor_imag = -damping * jnp.sin(phase_angle)
    wave_real, wave_imag = complex_scale(factor_real, factor_imag, wave[:, 0], wave[:, 1])
    angle_eye = jnp.eye(TH, dtype=jnp.float32)
    wave_real, wave_imag = complex_apply('kab,kxyb->kxya', angle_step[:, 0] + angle_eye, angle_step[:, 1], wave_real, wave_imag)
    stacked = jnp.stack((wave_real, wave_imag), axis=1)
    empty_block = jnp.zeros_like(stacked[:1])
    above_side = jnp.concatenate((stacked[1:], empty_block), axis=0)
    below_side = jnp.concatenate((empty_block, stacked[:KTOT - 1]), axis=0)
    helicity = jnp.arange(KTOT).astype(jnp.float32)
    top_value = float((KTOT - 1) * KTOT)
    coef_up = jnp.sqrt(top_value - helicity * (helicity + 1.0))
    coef_down = jnp.sqrt(top_value - (helicity - 1.0) * helicity)
    coupled = coef_up[:, None, None, None, None] * product('ab,kcxyb->kcxya', ladder, above_side)
    coupled = coupled + coef_down[:, None, None, None, None] * product('ba,kcxyb->kcxya', ladder, below_side)
    weight = coriolis_weight[None, :, None, None]
    wave_real = stacked[:, 0] + weight * coupled[:, 1]
    wave_imag = stacked[:, 1] - weight * coupled[:, 0]
    bond_eye = jnp.eye(RR, dtype=jnp.float32)
    wave_real, wave_imag = complex_apply('ab,kxbt->kxat', bond_step[0] + bond_eye, bond_step[1], wave_real, wave_imag)
    radial_eye = jnp.eye(R, dtype=jnp.float32)
    wave_real, wave_imag = complex_apply('ab,kbyt->kayt', radial_step[0] + radial_eye, radial_step[1], wave_real, wave_imag)
    wave_real, wave_imag = complex_scale(factor_real, factor_imag, wave_real, wave_imag)
    return jnp.stack((wave_real, wave_imag), axis=1).reshape(KTOT, 2, R, RR * TH)
```

```python
import functools
import math

import jax
import jax.numpy as jnp
from jax import lax
from jax.experimental import pallas as pl
from jax.experimental.pallas import tpu as pltpu
from jax.sharding import PartitionSpec as P

MESH = pl.DeviceIdType.MESH
VMEM = pltpu.VMEM
CHUNKS = 3
PAIR = 2
ROWS = 12
ANGLES = 96
f32, bf16 = jnp.float32, jnp.bfloat16


def split(x):
    high = x.astype(bf16)
    return high, (x - high.astype(f32)).astype(bf16)


def dot3(a, b, dims):
    def one(u, v):
        return lax.dot_general(u, v, (dims, ((), ())), preferred_element_type=f32)

    return one(a[0], b[0]) + (one(a[0], b[1]) + one(a[1], b[0]))


NN = ((1,), (0,))
NT = ((1,), (1,))


def lane(shape):
    return lax.broadcasted_iota(jnp.int32, shape, len(shape) - 1)


def sub(shape):
    return lax.broadcasted_iota(jnp.int32, shape, 0)


def lroll(x, n):
    return pltpu.roll(x, n, 1)


def sroll(x):
    return pltpu.roll(x, 4, 0)


def phase(half):
    s = half * half
    c = 1.0 / 479001600.0
    for k in (-1.0 / 3628800.0, 1.0 / 40320.0, -1.0 / 720.0, 1.0 / 24.0, -0.5, 1.0):
        c = c * s + k
    v = -1.0 / 39916800.0
    for k in (1.0 / 362880.0, -1.0 / 5040.0, 1.0 / 120.0, -1.0 / 6.0, 1.0):
        v = v * s + k
    return c, v * half


def spread(v0, v1, v2):
    n = lane(v0.shape)
    return (
        v0,
        lroll(jnp.where(n >= 96, v0, v1), 32),
        lroll(jnp.where(n >= 64, v1, v2), 64),
        lroll(v2, 96),
    )


def dense(b0, b1, b2, b3):
    n = lane(b0.shape)
    r1, r2, r3 = lroll(b1, 96), lroll(b2, 64), lroll(b3, 32)
    return jnp.where(n < 96, b0, r1), jnp.where(n < 64, r1, r2), jnp.where(n < 32, r2, r3)


def dense_half(u0, u1):
    n = lane(u0.shape)
    r = lroll(u1, 96)
    tail = jnp.where(n < 64, r, sroll(lroll(r, 64)))
    return jnp.where(n < 96, u0, r), tail[0:4]


def tail_rows(tail):
    both = jnp.concatenate([tail, tail], axis=0)
    return jnp.where(sub(both.shape) < 4, both, lroll(both, 64))


def spread_half(tile, tail):
    n = lane(tile.shape)
    return tile, lroll(jnp.where(n >= 96, tile, tail_rows(tail)), 32)


def angle_lanes(values):
    n = lane(values[0].shape[:-1] + (128,))
    a, b, c, d = values
    return jnp.where(n < 96, a, b), jnp.where(n < 64, b, c), jnp.where(n < 32, c, d)


def before_kernel(groups, wave, pot, ar, ab, bond, main, tail, pots, bigw, mat_hi, mat_lo):
    bonds = 4 * groups
    blocks = 3 * groups

    def turn(k, _):
        at = pl.ds(pl.multiple_of(k * 128, 128), 128)
        pots[pl.ds(k, 8, stride=blocks), :] = pot[0:8, at]
        pots[pl.ds(8 * blocks + k, 4, stride=blocks), :] = pot[8:12, at]
        return 0

    lax.fori_loop(0, blocks, turn, 0, unroll=4)

    place = lax.broadcasted_iota(jnp.int32, (bonds, bonds), 1)
    point = lax.broadcasted_iota(jnp.int32, (bonds, bonds), 0)
    perm = jnp.where(point == 4 * (place % groups) + place // groups, 1.0, 0.0).astype(bf16)
    for c in range(2):
        for part, mat in zip(split(bond[c]), (mat_hi, mat_lo)):
            cols = jnp.dot(part, perm, preferred_element_type=f32).astype(bf16)
            rows = lax.dot_general(perm, cols, (((0,), (0,)), ((), ())), preferred_element_type=f32)
            rows = rows.astype(bf16)
            if c == 0:
                mat[0:bonds, 0:bonds] = rows
                mat[bonds:, bonds:] = rows
            else:
                mat[0:bonds, bonds:] = -rows
                mat[bonds:, 0:bonds] = rows

    grid = (groups, bonds)
    cols = []
    for i in range(4):
        mine = jnp.where(lane(grid) == 4 * sub(grid) + i, jnp.broadcast_to(ab[...], grid), 0.0)
        cols.append(jnp.exp(-0.5 * jnp.sum(mine, axis=1, keepdims=True)))
    damp = angle_lanes([jnp.broadcast_to(c, (groups, 128)) for c in cols])
    decay = jnp.exp(-0.5 * ar[...])

    def two_rows(h, _):
        sides = []
        for k in range(2):
            r = 2 * h + k
            own = jnp.sum(jnp.where(lane((1, 128)) == r, decay, 0.0), axis=1, keepdims=True)
            re, im = [], []
            for i in range(3):
                x = wave[pl.ds(r * 2 * blocks + 2 * i, groups, stride=6), :]
                y = wave[pl.ds(r * 2 * blocks + 2 * i + 1, groups, stride=6), :]
                co, si = phase(0.5 * pots[pl.ds(r * blocks + i, groups, stride=3), :])
                d = damp[i] * own
                co, si = d * co, d * si
                re.append(co * x + si * y)
                im.append(co * y - si * x)
            sides.append(jnp.concatenate(spread(*re) + spread(*im), axis=0))
        x = jnp.concatenate(sides, axis=1)
        x = x + dot3((mat_hi[...], mat_lo[...]), split(x), NN)
        for k in range(2):
            r = 2 * h + k
            for c in range(2):
                row = jnp.where(r < 8, r + 8 * c, r + 8 + 4 * c)
                for i in range(4):
                    at = (4 * c + i) * groups
                    bigw[pl.ds(24 * i + row, groups, stride=96), :] = x[at : at + groups, 128 * k : 128 * k + 128]
        return 0

    lax.fori_loop(0, ROWS // 2, two_rows, 0)

    def pack(p, _):
        w = [[bigw[pl.ds(pl.multiple_of((2 * p + b) * 24, 8) + 8 * k, 8), :] for k in range(3)] for b in range(2)]
        t = dense(w[0][0], w[1][0], w[0][1], w[1][1])
        last, rest = dense_half(w[0][2], w[1][2])
        for k in range(3):
            main[p, 8 * k : 8 * k + 8, :] = t[k]
        main[p, 24:32, :] = last
        tail[p] = rest
        return 0

    lax.fori_loop(0, bonds // 2, pack, 0, unroll=2)


def turn_kernel(
    nz, top, sent_m, sent_t, weight, angle, ladder, radial, back_m, back_t,
    got_m, got_t, got_w, own_w, wide, work, from_up, from_down, reply_m, reply_t,
    a_hi, a_lo, u_hi, u_lo, d_hi, d_lo, r_hi, r_lo, scratch,
    angles, sa_sem, ra_sem, s1m, s1t, s1w, r1m, r1t, r1w, su, sd, ru, rd, s2m, s2t, r2m, r2t,
):
    owners = 4 * nz
    ka, sa = lax.axis_index("ka"), lax.axis_index("sa")
    x, yh = ka // 2, ka % 2
    yl, z, core = sa // (2 * nz), (sa // 2) % nz, sa % 2
    y = 2 * yh + yl
    helicity = 2 * x + core
    me_owner = y * nz + z
    at_home = core == yh

    def owner_of(q, c):
        oy, oz = q // nz, q % nz
        return (2 * x + oy // 2, (oy % 2) * (2 * nz) + oz * 2 + c)

    def home_of(s):
        return (2 * x + core, s)

    def turned(i):
        return ((y + i % 4) % 4) * nz + (z + nz // 2 + i // 4) % nz

    def turned_home(i):
        c, iy, iz = i % 2, (i // 2) % 2, i // 4
        return ((yl + iy) % 2) * (2 * nz) + ((z + nz // 2 + iz) % nz) * 2 + c

    has_up, has_down = helicity < top, helicity > 0
    kx_up = jnp.where(core == 0, x, x + 1)
    kx_down = jnp.where(core == 1, x, x - 1)
    up_dev = (2 * kx_up + yh, yl * (2 * nz) + z * 2 + 1 - core)
    down_dev = (2 * kx_down + yh, yl * (2 * nz) + z * 2 + 1 - core)

    barrier = pltpu.get_barrier_semaphore()

    def greet(i, _):
        q, s = turned(i), turned_home(i)

        @pl.when(jnp.logical_not(at_home & (q == me_owner)))
        def _():
            pl.semaphore_signal(barrier, inc=1, device_id=owner_of(q, yh), device_id_type=MESH)

        @pl.when(jnp.logical_not(at_home & (s == sa)))
        def _():
            pl.semaphore_signal(barrier, inc=1, device_id=home_of(s), device_id_type=MESH)

        return 0

    lax.fori_loop(0, owners, greet, 0)

    @pl.when(has_up)
    def _():
        pl.semaphore_signal(barrier, inc=1, device_id=up_dev, device_id_type=MESH)

    @pl.when(has_down)
    def _():
        pl.semaphore_signal(barrier, inc=1, device_id=down_dev, device_id_type=MESH)

    own_w[...] = weight[...]

    expected = 2 * owners - 2 * at_home.astype(jnp.int32)
    expected = expected + has_up.astype(jnp.int32) + has_down.astype(jnp.int32)
    pl.semaphore_wait(barrier, expected)

    def send_chunk(j, src_m, src_t, dst_m, dst_t, pick, device, slot, ssm, sst, rsm, rst, self_slot):
        def one(i, _):
            q = pick(i)
            mine = at_home & (q == self_slot)
            here = [
                (src_m.at[j * owners + q], dst_m.at[j * owners + slot], ssm.at[j], rsm.at[j]),
                (src_t.at[j * owners + q], dst_t.at[j * owners + slot], sst.at[j], rst.at[j]),
            ]

            @pl.when(mine)
            def _():
                for a, b, _, r in here:
                    pltpu.make_async_copy(a, b, r).start()

            @pl.when(jnp.logical_not(mine))
            def _():
                for a, b, s, r in here:
                    pltpu.make_async_remote_copy(
                        src_ref=a, dst_ref=b, send_sem=s, recv_sem=r, device_id=device(q), device_id_type=MESH
                    ).start()

            return 0

        lax.fori_loop(0, owners, one, 0)

    def send_weight(i, _):
        q = turned(i)
        mine = at_home & (q == me_owner)

        @pl.when(mine)
        def _():
            pltpu.make_async_copy(own_w, got_w.at[sa], r1w).start()

        @pl.when(jnp.logical_not(mine))
        def _():
            pltpu.make_async_remote_copy(
                src_ref=own_w, dst_ref=got_w.at[sa], send_sem=s1w, recv_sem=r1w,
                device_id=owner_of(q, yh), device_id_type=MESH,
            ).start()

        return 0

    def wait_bytes(ref, count, start, sem):
        view = ref.at[pl.ds(start, count)]
        pltpu.make_async_copy(view, view, sem).wait()

    def wait_sent(ref, start, sem):
        @pl.when(at_home)
        def _():
            wait_bytes(ref, owners - 1, start, sem)

        @pl.when(jnp.logical_not(at_home))
        def _():
            wait_bytes(ref, owners, start, sem)

    to_other = pltpu.make_async_remote_copy(
        src_ref=angle, dst_ref=angles, send_sem=sa_sem, recv_sem=ra_sem,
        device_id=(2 * x + 1 - yh, sa), device_id_type=MESH,
    )

    @pl.when(at_home)
    def _():
        to_other.start()
        angles[...] = angle[...]

    lax.fori_loop(0, owners, send_weight, 0)
    for j in range(CHUNKS):
        send_chunk(
            j, sent_m, sent_t, got_m, got_t, turned, lambda q: owner_of(q, yh), sa, s1m, s1t, r1m, r1t, me_owner
        )

    def fill(parts, hi, lo, shape):
        scratch[0 : shape[0], 0 : shape[1]] = jnp.zeros(shape, f32)
        for row, col, value in parts:
            scratch[row : row + ANGLES, col : col + ANGLES] = value
        high, low = split(scratch[0 : shape[0], 0 : shape[1]])
        hi[...] = high
        lo[...] = low

    coef_up, coef_down = 0.0, 0.0
    for k in range(top + 1):
        coef_up = jnp.where(helicity == k, math.sqrt(top * (top + 1) - k * (k + 1)), coef_up)
        coef_down = jnp.where(helicity == k, math.sqrt(top * (top + 1) - (k - 1) * k), coef_down)
    up = coef_up * ladder[...]
    down = coef_down * ladder[...]
    fill([(0, 128, up), (128, 0, -up)], u_hi, u_lo, (256, 256))
    fill([(128, 0, down), (0, 128, -down)], d_hi, d_lo, (256, 256))
    count = radial.shape[1]
    for c in range(2):
        high, low = split(radial[c])
        for part, mat in ((high, r_hi), (low, r_lo)):
            if c == 0:
                mat[0:count, 0:count] = part
                mat[count:, count:] = part
            else:
                mat[0:count, count:] = -part
                mat[count:, 0:count] = part

    for buf, has in ((from_up, has_up), (from_down, has_down)):

        @pl.when(jnp.logical_not(has))
        def _(buf=buf):
            buf[...] = jnp.zeros(buf.shape, f32)

    @pl.when(jnp.logical_not(at_home))
    def _():
        to_other.wait_recv()

    fill(
        [(0, 0, angles[0, 0]), (128, 128, angles[0, 0]), (0, 128, -angles[0, 1]), (128, 0, angles[0, 1])],
        a_hi, a_lo, (256, 256),
    )
    wait_bytes(got_w, owners, 0, r1w)

    def weights(sp, _):
        shape = (2 * ROWS, 128)
        row = sub(shape)
        a = jnp.where(row < ROWS, got_w[2 * sp], got_w[2 * sp + 1])
        a = jnp.where(lane(shape) == jnp.where(row < ROWS, row, row - ROWS), a, 0.0)
        at = pl.ds(pl.multiple_of(sp * 2 * ROWS, 8), 2 * ROWS)
        wide[at, :] = jnp.broadcast_to(jnp.sum(a, axis=1, keepdims=True), shape)
        return 0

    lax.fori_loop(0, owners // 2, weights, 0)

    for j in range(CHUNKS):
        wait_bytes(got_m, owners, j * owners, r1m.at[j])
        wait_bytes(got_t, owners, j * owners, r1t.at[j])

        def unpack(sp, _, j=j):
            top8 = sub((8, 128)) < 4
            got = []
            for k in range(2):
                s = j * owners + 2 * sp + k
                t = [got_m[s, 8 * i : 8 * i + 8, :] for i in range(4)]
                re0, re1, im0, im1 = spread(t[0], t[1], t[2])
                u0, u1 = spread_half(t[3], got_t[s])
                got.append(((re0, im0, u0), (re1, im1, u1)))
            base = pl.multiple_of(sp * 24, 8)
            for b in range(2):
                (re_a, im_a, u_a), (re_b, im_b, u_b) = got[0][b], got[1][b]
                re_b, im_b = sroll(re_b), sroll(im_b)
                tiles = (
                    (re_a, jnp.where(top8, u_a, re_b), jnp.where(top8, re_b, sroll(u_b))),
                    (im_a, jnp.where(top8, sroll(u_a), im_b), jnp.where(top8, im_b, u_b)),
                )
                for c in range(2):
                    for i in range(3):
                        work[j, b, pl.ds(base + 8 * i, 8), 128 * c : 128 * c + 128] = tiles[c][i]
            return 0

        lax.fori_loop(0, owners // 2, unpack, 0)
        for b in range(2):
            v = work[j, b]
            work[j, b] = v + dot3(split(v), (a_hi[...], a_lo[...]), NT)

        @pl.when(has_up)
        def _(j=j):
            pltpu.make_async_remote_copy(
                src_ref=work.at[j], dst_ref=from_down.at[j], send_sem=su.at[j], recv_sem=rd.at[j],
                device_id=up_dev, device_id_type=MESH,
            ).start()

        @pl.when(has_down)
        def _(j=j):
            pltpu.make_async_remote_copy(
                src_ref=work.at[j], dst_ref=from_up.at[j], send_sem=sd.at[j], recv_sem=ru.at[j],
                device_id=down_dev, device_id_type=MESH,
            ).start()

        @pl.when(has_up)
        def _(j=j):
            pltpu.make_async_copy(from_up.at[j], from_up.at[j], ru.at[j]).wait()

        @pl.when(has_down)
        def _(j=j):
            pltpu.make_async_copy(from_down.at[j], from_down.at[j], rd.at[j]).wait()

        third = []
        for b in range(2):
            c = dot3(split(from_up[j, b]), (u_hi[...], u_lo[...]), NT)
            c = c + dot3(split(from_down[j, b]), (d_hi[...], d_lo[...]), NN)
            w = wide[...]
            third.append(work[j, b] + jnp.concatenate([w, w], axis=1) * c)
        v = jnp.concatenate(
            [
                jnp.concatenate([third[0][:, 0:128], third[1][:, 0:128]], axis=1),
                jnp.concatenate([third[0][:, 128:256], third[1][:, 128:256]], axis=1),
            ],
            axis=0,
        )
        scratch[...] = v + dot3((r_hi[...], r_lo[...]), split(v), NN)

        def repack(sp, _, j=j):
            top8 = sub((8, 128)) < 4
            base = pl.multiple_of(sp * 24, 8)
            out = [[], []]
            for b in range(2):
                (a0, a1, a2), (i0, i1, i2) = [
                    [scratch[pl.ds(base + c * count + 8 * i, 8), 128 * b : 128 * b + 128] for i in range(3)]
                    for c in range(2)
                ]
                r1, r2, q1, q2 = sroll(a1), sroll(a2), sroll(i1), sroll(i2)
                out[0].append((a0, i0, jnp.where(top8, a1, q1)))
                out[1].append((jnp.where(top8, r1, r2), jnp.where(top8, q1, q2), jnp.where(top8, r2, i2)))
            for k in range(2):
                s = j * owners + 2 * sp + k
                (re0, im0, u0), (re1, im1, u1) = out[k]
                t = dense(re0, re1, im0, im1)
                last, rest = dense_half(u0, u1)
                for i in range(3):
                    reply_m[s, 8 * i : 8 * i + 8, :] = t[i]
                reply_m[s, 24:32, :] = last
                reply_t[s] = rest
            return 0

        lax.fori_loop(0, owners // 2, repack, 0)
        send_chunk(
            j, reply_m, reply_t, back_m, back_t, turned_home, home_of, me_owner, s2m, s2t, r2m, r2t, sa
        )

    @pl.when(at_home)
    def _():
        to_other.wait_send()

    wait_sent(got_w, 0, s1w)
    for j in range(CHUNKS):
        wait_sent(sent_m, j * owners, s1m.at[j])
        wait_sent(sent_t, j * owners, s1t.at[j])

        @pl.when(has_up)
        def _(j=j):
            pltpu.make_async_copy(work.at[j], work.at[j], su.at[j]).wait()

        @pl.when(has_down)
        def _(j=j):
            pltpu.make_async_copy(work.at[j], work.at[j], sd.at[j]).wait()

    for j in range(CHUNKS):
        wait_bytes(back_m, owners, j * owners, r2m.at[j])
        wait_bytes(back_t, owners, j * owners, r2t.at[j])
        wait_sent(reply_m, j * owners, s2m.at[j])
        wait_sent(reply_t, j * owners, s2t.at[j])


def after_kernel(groups, main, tail, pot, ar, ab, out):
    blocks = 3 * groups
    row8 = sub((8, 1))
    decay8, decay4 = jnp.zeros((8, 1), f32), jnp.zeros((8, 1), f32)
    for k in range(8):
        decay8 = jnp.where(row8 == k, ar[k], decay8)
        decay4 = jnp.where(row8 % 4 == k % 4, ar[8 + k % 4], decay4)

    def group(g, _):
        points = [jnp.full((8, 128), ab[4 * g + i], f32) for i in range(4)]
        flat = angle_lanes(points)
        a, b = 2 * g, 2 * g + 1
        ta = [main[a, 8 * i : 8 * i + 8, :] for i in range(4)]
        tb = [main[b, 8 * i : 8 * i + 8, :] for i in range(4)]
        low = lane((8, 128)) < 64
        b0, b1, b3 = lroll(tb[0], 64), lroll(tb[1], 64), lroll(tb[3], 64)
        a1, a2 = lroll(ta[1], 64), lroll(ta[2], 64)
        re = (ta[0], jnp.where(low, ta[1], b0), jnp.where(low, b0, b1))
        im = (jnp.where(low, a1, a2), jnp.where(low, a2, tb[1]), tb[2])
        ra, rb = tail_rows(tail[a]), tail_rows(tail[b])
        u = (ta[3], jnp.where(low, ra, b3), jnp.where(low, b3, lroll(rb, 64)))
        top = sub((8, 128)) < 4
        for i in range(3):
            k = 3 * g + i
            at = pl.ds(pl.multiple_of(k * 128, 128), 128)
            co, si = phase(0.5 * pot[0:8, at])
            d = jnp.exp(-0.5 * (decay8 + flat[i]))
            co, si = d * co, d * si
            out[pl.ds(2 * k, 8, stride=2 * blocks), :] = co * re[i] + si * im[i]
            out[pl.ds(2 * k + 1, 8, stride=2 * blocks), :] = co * im[i] - si * re[i]
            p4 = pot[8:12, at]
            co, si = phase(0.5 * jnp.concatenate([p4, p4], axis=0))
            d = jnp.exp(-0.5 * (decay4 + flat[i]))
            co, si = d * co, d * si
            v = co * u[i] + jnp.where(top, si, -si) * sroll(u[i])
            out[pl.ds(16 * blocks + 2 * k, 4, stride=2 * blocks), :] = v[0:4]
            out[pl.ds(16 * blocks + 2 * k + 1, 4, stride=2 * blocks), :] = v[4:8]
        return 0

    lax.fori_loop(0, groups, group, 0)


def body(wave_in, potential, absorb_radial, absorb_bond, coriolis_weight, ladder, angle_step, bond_step, radial_step):
    rows, columns = wave_in.shape[2:]
    blocks = columns // 128
    groups = blocks // 3
    nz = lax.axis_size("sa") // 4
    owners = 4 * nz
    top = lax.axis_size("ka") - 1
    count = radial_step.shape[1]
    full = pl.BlockSpec(memory_space=VMEM)
    smem = pl.BlockSpec(memory_space=pltpu.SMEM)
    hbm = pl.BlockSpec(memory_space=pl.ANY)
    shape = jax.ShapeDtypeStruct
    wave = wave_in.reshape(2, rows, blocks, 128).transpose(1, 2, 0, 3).reshape(rows * blocks * 2, 128)
    pad = jnp.pad(absorb_radial, (0, 128 - rows)).reshape(1, 128)
    weight = jnp.pad(coriolis_weight, (0, 128 - rows)).reshape(1, 128)
    messages = CHUNKS * owners
    main, tail = pl.pallas_call(
        functools.partial(before_kernel, groups),
        out_shape=(shape((messages, 32, 128), f32), shape((messages, 4, 128), f32)),
        in_specs=[full] * 5,
        out_specs=(full, full),
        scratch_shapes=[
            VMEM((rows * blocks, 128), f32),
            VMEM((96 * groups, 128), f32),
            VMEM((8 * groups, 8 * groups), bf16),
            VMEM((8 * groups, 8 * groups), bf16),
        ],
        compiler_params=pltpu.CompilerParams(vmem_limit_bytes=50 << 20),
        name="before",
    )(wave, potential, pad, absorb_bond.reshape(1, -1), bond_step)
    dma, many = pltpu.SemaphoreType.DMA, pltpu.SemaphoreType.DMA((CHUNKS,))
    back_m, back_t = pl.pallas_call(
        functools.partial(turn_kernel, nz, top),
        out_shape=(shape((messages, 32, 128), f32), shape((messages, 4, 128), f32)),
        in_specs=[hbm, hbm, full, full, full, full],
        out_specs=(hbm, hbm),
        scratch_shapes=[
            VMEM((messages, 32, 128), f32),
            VMEM((messages, 4, 128), f32),
            VMEM((owners, 1, 128), f32),
            VMEM((1, 128), f32),
            VMEM((count, 128), f32),
            VMEM((CHUNKS, 2, count, 256), f32),
            VMEM((CHUNKS, 2, count, 256), f32),
            VMEM((CHUNKS, 2, count, 256), f32),
            VMEM((messages, 32, 128), f32),
            VMEM((messages, 4, 128), f32),
            VMEM((256, 256), bf16),
            VMEM((256, 256), bf16),
            VMEM((256, 256), bf16),
            VMEM((256, 256), bf16),
            VMEM((256, 256), bf16),
            VMEM((256, 256), bf16),
            VMEM((2 * count, 2 * count), bf16),
            VMEM((2 * count, 2 * count), bf16),
            VMEM((2 * count, 256), f32),
            VMEM((1, 2, ANGLES, ANGLES), f32), dma, dma,
            many, many, dma, many, many, dma,
            many, many, many, many,
            many, many, many, many,
        ],
        compiler_params=pltpu.CompilerParams(collective_id=0, has_side_effects=True, vmem_limit_bytes=50 << 20),
        name="turn",
    )(main, tail, weight, angle_step, ladder, radial_step)
    out = pl.pallas_call(
        functools.partial(after_kernel, groups),
        out_shape=shape((rows * blocks * 2, 128), f32),
        in_specs=[full, full, full, smem, smem],
        out_specs=full,
        compiler_params=pltpu.CompilerParams(vmem_limit_bytes=50 << 20),
        name="after",
    )(back_m, back_t, potential, absorb_radial, absorb_bond)
    return out.reshape(rows, blocks, 2, 128).transpose(2, 0, 1, 3).reshape(1, 2, rows, columns)


def solution(mesh):
    return jax.shard_map(
        body,
        mesh=mesh,
        in_specs=(
            P("ka", None, "sa", None),
            P("sa", None),
            P("sa"),
            P(),
            P("sa"),
            P(),
            P("ka", None, None, None),
            P(),
            P(),
        ),
        out_specs=P("ka", None, "sa", None),
        check_vma=False,
    )
```

```python
import functools
import math

import jax
import jax.numpy as jnp
from jax import lax
from jax.experimental import pallas as pl
from jax.experimental.pallas import tpu as pltpu
from jax.sharding import PartitionSpec as P

MESH = pl.DeviceIdType.MESH
VMEM = pltpu.VMEM
CHUNKS = 3
PAIR = 2
ROWS = 12
ANGLES = 96
PACK = 4
GATES = 4
f32, bf16 = jnp.float32, jnp.bfloat16


def split(x):
    high = x.astype(bf16)
    return high, (x - high.astype(f32)).astype(bf16)


def dot3(a, b, dims):
    def one(u, v):
        return lax.dot_general(u, v, (dims, ((), ())), preferred_element_type=f32)

    return one(a[0], b[0]) + (one(a[0], b[1]) + one(a[1], b[0]))


NN = ((1,), (0,))
NT = ((1,), (1,))


def lane(shape):
    return lax.broadcasted_iota(jnp.int32, shape, len(shape) - 1)


def sub(shape):
    return lax.broadcasted_iota(jnp.int32, shape, 0)


def lroll(x, n):
    return pltpu.roll(x, n, 1)


def sroll(x):
    return pltpu.roll(x, 4, 0)


def phase(half):
    s = half * half
    c = 1.0 / 479001600.0
    for k in (-1.0 / 3628800.0, 1.0 / 40320.0, -1.0 / 720.0, 1.0 / 24.0, -0.5, 1.0):
        c = c * s + k
    v = -1.0 / 39916800.0
    for k in (1.0 / 362880.0, -1.0 / 5040.0, 1.0 / 120.0, -1.0 / 6.0, 1.0):
        v = v * s + k
    return c, v * half


def spread(v0, v1, v2):
    n = lane(v0.shape)
    return (
        v0,
        lroll(jnp.where(n >= 96, v0, v1), 32),
        lroll(jnp.where(n >= 64, v1, v2), 64),
        lroll(v2, 96),
    )


def dense(b0, b1, b2, b3):
    n = lane(b0.shape)
    r1, r2, r3 = lroll(b1, 96), lroll(b2, 64), lroll(b3, 32)
    return jnp.where(n < 96, b0, r1), jnp.where(n < 64, r1, r2), jnp.where(n < 32, r2, r3)


def dense_half(u0, u1):
    n = lane(u0.shape)
    r = lroll(u1, 96)
    tail = jnp.where(n < 64, r, sroll(lroll(r, 64)))
    return jnp.where(n < 96, u0, r), tail[0:4]


def tail_rows(tail):
    both = jnp.concatenate([tail, tail], axis=0)
    return jnp.where(sub(both.shape) < 4, both, lroll(both, 64))


def spread_half(tile, tail):
    n = lane(tile.shape)
    return tile, lroll(jnp.where(n >= 96, tile, tail_rows(tail)), 32)


def angle_lanes(values):
    n = lane(values[0].shape[:-1] + (128,))
    a, b, c, d = values
    return jnp.where(n < 96, a, b), jnp.where(n < 64, b, c), jnp.where(n < 32, c, d)


def before_kernel(groups, wave, pot, ar, ab, bond, main, tail, pots, bigw, mat_hi, mat_lo):
    bonds = 4 * groups
    blocks = 3 * groups
    pitch = blocks + 1

    def turn(k, _):
        at = pl.ds(pl.multiple_of(k * 128, 128), 128)
        pots[pl.ds(k, 8, stride=pitch), :] = pot[0:8, at]
        pots[pl.ds(8 * pitch + k, 4, stride=pitch), :] = pot[8:12, at]
        return 0

    lax.fori_loop(0, blocks, turn, 0, unroll=4)

    place = lax.broadcasted_iota(jnp.int32, (bonds, bonds), 1)
    point = lax.broadcasted_iota(jnp.int32, (bonds, bonds), 0)
    perm = jnp.where(point == 4 * (place % groups) + place // groups, 1.0, 0.0).astype(bf16)
    for c in range(2):
        for part, mat in zip(split(bond[c]), (mat_hi, mat_lo)):
            cols = jnp.dot(part, perm, preferred_element_type=f32).astype(bf16)
            rows = lax.dot_general(perm, cols, (((0,), (0,)), ((), ())), preferred_element_type=f32)
            rows = rows.astype(bf16)
            if c == 0:
                mat[0:bonds, 0:bonds] = rows
                mat[bonds:, bonds:] = rows
            else:
                mat[0:bonds, bonds:] = -rows
                mat[bonds:, 0:bonds] = rows

    grid = (groups, bonds)
    cols = []
    for i in range(4):
        mine = jnp.where(lane(grid) == 4 * sub(grid) + i, jnp.broadcast_to(ab[...], grid), 0.0)
        cols.append(jnp.exp(-0.5 * jnp.sum(mine, axis=1, keepdims=True)))
    damp = angle_lanes([jnp.broadcast_to(c, (groups, 128)) for c in cols])
    decay = jnp.exp(-0.5 * ar[...])

    def two_rows(h, _):
        sides = []
        for k in range(2):
            r = 2 * h + k
            own = jnp.sum(jnp.where(lane((1, 128)) == r, decay, 0.0), axis=1, keepdims=True)
            re, im = [], []
            for i in range(3):
                x = wave[pl.ds(r * 2 * blocks + 2 * i, groups, stride=6), :]
                y = wave[pl.ds(r * 2 * blocks + 2 * i + 1, groups, stride=6), :]
                co, si = phase(0.5 * pots[pl.ds(r * pitch + i, groups, stride=3), :])
                d = damp[i] * own
                co, si = d * co, d * si
                re.append(co * x + si * y)
                im.append(co * y - si * x)
            sides.append(jnp.concatenate(spread(*re) + spread(*im), axis=0))
        x = jnp.concatenate(sides, axis=1)
        x = x + dot3((mat_hi[...], mat_lo[...]), split(x), NN)
        for k in range(2):
            r = 2 * h + k
            for c in range(2):
                row = jnp.where(r < 8, r + 8 * c, r + 8 + 4 * c)
                for i in range(4):
                    at = (4 * c + i) * groups
                    bigw[pl.ds(i + 5 * row, groups, stride=121), :] = x[at : at + groups, 128 * k : 128 * k + 128]
        return 0

    lax.fori_loop(0, ROWS // 2, two_rows, 0, unroll=True)

    def pack(h, _):
        pairs = [PACK * h + k for k in range(PACK)]
        loaded = [
            [bigw[pl.ds(121 * (p // 2) + 2 * (p % 2) + b + 40 * k, 8, stride=5), :] for b in range(2) for k in range(3)]
            for p in pairs
        ]
        made = [
            (*dense(w[0], w[3], w[1], w[4]), *dense_half(w[2], w[5])) for w in loaded
        ]
        for p, t in zip(pairs, made):
            for k in range(4):
                main[p, 8 * k : 8 * k + 8, :] = t[k]
            tail[p] = t[4]
        return 0

    lax.fori_loop(0, bonds // 2 // PACK, pack, 0, unroll=2)


def turn_kernel(
    nz, top, sent_m, sent_t, weight, angle, ladder, radial, back_m, back_t,
    got_m, got_t, got_w, own_w, wide, work, from_up, from_down, reply_m, reply_t,
    a_hi, a_lo, u_hi, u_lo, d_hi, d_lo, r_hi, r_lo, scratch,
    angles, sa_sem, ra_sem, s1m, s1t, s1w, r1m, r1t, r1w, su, sd, ru, rd, s2m, s2t, r2m, r2t,
):
    owners = 4 * nz
    ka, sa = lax.axis_index("ka"), lax.axis_index("sa")
    x, yh = ka // 2, ka % 2
    yl, z, core = sa // (2 * nz), (sa // 2) % nz, sa % 2
    y = 2 * yh + yl
    helicity = 2 * x + core
    me_owner = y * nz + z
    at_home = core == yh

    def owner_of(q, c):
        oy, oz = q // nz, q % nz
        return (2 * x + oy // 2, (oy % 2) * (2 * nz) + oz * 2 + c)

    def home_of(s):
        return (2 * x + core, s)

    def turned(i):
        return ((y + i % 4) % 4) * nz + (z + nz // 2 + i // 4) % nz

    def turned_home(i):
        c, iy, iz = i % 2, (i // 2) % 2, i // 4
        return ((yl + iy) % 2) * (2 * nz) + ((z + nz // 2 + iz) % nz) * 2 + c

    has_up, has_down = helicity < top, helicity > 0
    kx_up = jnp.where(core == 0, x, x + 1)
    kx_down = jnp.where(core == 1, x, x - 1)
    up_dev = (2 * kx_up + yh, yl * (2 * nz) + z * 2 + 1 - core)
    down_dev = (2 * kx_down + yh, yl * (2 * nz) + z * 2 + 1 - core)

    barrier = pltpu.get_barrier_semaphore()

    def greet(i, _):
        q, s = turned(i), turned_home(i)

        @pl.when(jnp.logical_not(at_home & (q == me_owner)))
        def _():
            pl.semaphore_signal(barrier, inc=1, device_id=owner_of(q, yh), device_id_type=MESH)

        @pl.when(jnp.logical_not(at_home & (s == sa)))
        def _():
            pl.semaphore_signal(barrier, inc=1, device_id=home_of(s), device_id_type=MESH)

        return 0

    lax.fori_loop(0, owners, greet, 0)

    @pl.when(has_up)
    def _():
        pl.semaphore_signal(barrier, inc=1, device_id=up_dev, device_id_type=MESH)

    @pl.when(has_down)
    def _():
        pl.semaphore_signal(barrier, inc=1, device_id=down_dev, device_id_type=MESH)

    own_w[...] = weight[...]

    expected = 2 * owners - 2 * at_home.astype(jnp.int32)
    expected = expected + has_up.astype(jnp.int32) + has_down.astype(jnp.int32)
    pl.semaphore_wait(barrier, expected)

    def send_chunk(j, part, src_m, src_t, dst_m, dst_t, pick, device, slot, ssm, sst, rsm, rst, self_slot):
        def one(i, _):
            q = pick(i)
            mine = at_home & (q == self_slot)
            here = [
                (src_m.at[j * owners + q], dst_m.at[j * owners + slot], ssm, rsm.at[j]),
                (src_t.at[j * owners + q], dst_t.at[j * owners + slot], sst.at[j], rst.at[j]),
            ]

            @pl.when(mine)
            def _():
                for a, b, _, r in here:
                    pltpu.make_async_copy(a, b, r).start()

            @pl.when(jnp.logical_not(mine))
            def _():
                for a, b, s, r in here:
                    pltpu.make_async_remote_copy(
                        src_ref=a, dst_ref=b, send_sem=s, recv_sem=r, device_id=device(q), device_id_type=MESH
                    ).start()

            return 0

        lax.fori_loop(*part, one, 0)

    def send_weight(i, _):
        q = turned(i)
        mine = at_home & (q == me_owner)

        @pl.when(mine)
        def _():
            pltpu.make_async_copy(own_w, got_w.at[sa], r1w).start()

        @pl.when(jnp.logical_not(mine))
        def _():
            pltpu.make_async_remote_copy(
                src_ref=own_w, dst_ref=got_w.at[sa], send_sem=s1w, recv_sem=r1w,
                device_id=owner_of(q, yh), device_id_type=MESH,
            ).start()

        return 0

    def wait_bytes(ref, count, start, sem):
        view = ref.at[pl.ds(start, count)]
        pltpu.make_async_copy(view, view, sem).wait()

    def wait_sent(ref, start, sem):
        @pl.when(at_home)
        def _():
            wait_bytes(ref, owners - 1, start, sem)

        @pl.when(jnp.logical_not(at_home))
        def _():
            wait_bytes(ref, owners, start, sem)

    to_other = pltpu.make_async_remote_copy(
        src_ref=angle, dst_ref=angles, send_sem=sa_sem, recv_sem=ra_sem,
        device_id=(2 * x + 1 - yh, sa), device_id_type=MESH,
    )

    @pl.when(at_home)
    def _():
        to_other.start()
        angles[...] = angle[...]

    lax.fori_loop(0, owners, send_weight, 0)
    size = owners // GATES
    mine_at = (nz // 2) * 4 // size

    def first_send(j, k):
        send_chunk(
            j, (k * size, k * size + size), sent_m, sent_t, got_m, got_t, turned, lambda q: owner_of(q, yh), sa,
            s1m.at[j, k], s1t, r1m, r1t, me_owner,
        )

    def gate(j, k):
        if k != mine_at:
            wait_bytes(sent_m, size, 0, s1m.at[j, k])
        else:

            @pl.when(at_home)
            def _():
                wait_bytes(sent_m, size - 1, 0, s1m.at[j, k])

            @pl.when(jnp.logical_not(at_home))
            def _():
                wait_bytes(sent_m, size, 0, s1m.at[j, k])

    def advance(j, parts):
        for k in parts:
            if j < CHUNKS:
                gate(j, k)
            if j + 1 < CHUNKS:
                first_send(j + 1, k)

    for k in range(GATES):
        first_send(0, k)

    def fill(parts, hi, lo, shape):
        scratch[0 : shape[0], 0 : shape[1]] = jnp.zeros(shape, f32)
        for row, col, value in parts:
            scratch[row : row + ANGLES, col : col + ANGLES] = value
        high, low = split(scratch[0 : shape[0], 0 : shape[1]])
        hi[...] = high
        lo[...] = low

    coef_up, coef_down = 0.0, 0.0
    for k in range(top + 1):
        coef_up = jnp.where(helicity == k, math.sqrt(top * (top + 1) - k * (k + 1)), coef_up)
        coef_down = jnp.where(helicity == k, math.sqrt(top * (top + 1) - (k - 1) * k), coef_down)
    up = coef_up * ladder[...]
    down = coef_down * ladder[...]
    fill([(0, 128, up), (128, 0, -up)], u_hi, u_lo, (256, 256))
    fill([(128, 0, down), (0, 128, -down)], d_hi, d_lo, (256, 256))
    count = radial.shape[1]
    for c in range(2):
        high, low = split(radial[c])
        for part, mat in ((high, r_hi), (low, r_lo)):
            if c == 0:
                mat[0:count, 0:count] = part
                mat[count:, count:] = part
            else:
                mat[0:count, count:] = -part
                mat[count:, 0:count] = part

    for buf, has in ((from_up, has_up), (from_down, has_down)):

        @pl.when(jnp.logical_not(has))
        def _(buf=buf):
            buf[...] = jnp.zeros(buf.shape, f32)

    @pl.when(jnp.logical_not(at_home))
    def _():
        to_other.wait_recv()

    fill(
        [(0, 0, angles[0, 0]), (128, 128, angles[0, 0]), (0, 128, -angles[0, 1]), (128, 0, angles[0, 1])],
        a_hi, a_lo, (256, 256),
    )
    wait_bytes(got_w, owners, 0, r1w)

    def weights(sp, _):
        shape = (2 * ROWS, 128)
        row = sub(shape)
        a = jnp.where(row < ROWS, got_w[2 * sp], got_w[2 * sp + 1])
        a = jnp.where(lane(shape) == jnp.where(row < ROWS, row, row - ROWS), a, 0.0)
        at = pl.ds(pl.multiple_of(sp * 2 * ROWS, 8), 2 * ROWS)
        wide[at, :] = jnp.broadcast_to(jnp.sum(a, axis=1, keepdims=True), shape)
        return 0

    lax.fori_loop(0, owners // 2, weights, 0)

    def receive(j):
        wait_bytes(got_m, owners, j * owners, r1m.at[j])
        wait_bytes(got_t, owners, j * owners, r1t.at[j])

        def unpack(h, _):
            top8 = sub((8, 128)) < 4
            loaded = [
                [got_m[j * owners + 4 * h + k, 8 * i : 8 * i + 8, :] for i in range(4)] + [got_t[j * owners + 4 * h + k]]
                for k in range(4)
            ]
            got = []
            for t in loaded:
                re0, re1, im0, im1 = spread(t[0], t[1], t[2])
                u0, u1 = spread_half(t[3], t[4])
                got.append(((re0, im0, u0), (re1, im1, u1)))
            made = []
            for sp in range(2):
                for b in range(2):
                    (re_a, im_a, u_a), (re_b, im_b, u_b) = got[2 * sp][b], got[2 * sp + 1][b]
                    re_b, im_b = sroll(re_b), sroll(im_b)
                    tiles = (
                        (re_a, jnp.where(top8, u_a, re_b), jnp.where(top8, re_b, sroll(u_b))),
                        (im_a, jnp.where(top8, sroll(u_a), im_b), jnp.where(top8, im_b, u_b)),
                    )
                    made += [(24 * sp + 8 * i, b, c, tiles[c][i]) for c in range(2) for i in range(3)]
            base = pl.multiple_of(h * 48, 8)
            for at, b, c, tile in made:
                work[j, b, pl.ds(base + at, 8), 128 * c : 128 * c + 128] = tile
            return 0

        lax.fori_loop(0, owners // 4, unpack, 0, unroll=2)
        for b in range(2):
            v = work[j, b]
            work[j, b] = v + dot3(split(v), (a_hi[...], a_lo[...]), NT)

        @pl.when(has_up)
        def _():
            pltpu.make_async_remote_copy(
                src_ref=work.at[j], dst_ref=from_down.at[j], send_sem=su.at[j], recv_sem=rd.at[j],
                device_id=up_dev, device_id_type=MESH,
            ).start()

        @pl.when(has_down)
        def _():
            pltpu.make_async_remote_copy(
                src_ref=work.at[j], dst_ref=from_up.at[j], send_sem=sd.at[j], recv_sem=ru.at[j],
                device_id=down_dev, device_id_type=MESH,
            ).start()


    def finish(j):
        @pl.when(has_up)
        def _():
            pltpu.make_async_copy(from_up.at[j], from_up.at[j], ru.at[j]).wait()

        @pl.when(has_down)
        def _():
            pltpu.make_async_copy(from_down.at[j], from_down.at[j], rd.at[j]).wait()

        third = []
        for b in range(2):
            c = dot3(split(from_up[j, b]), (u_hi[...], u_lo[...]), NT)
            c = c + dot3(split(from_down[j, b]), (d_hi[...], d_lo[...]), NN)
            w = wide[...]
            third.append(work[j, b] + jnp.concatenate([w, w], axis=1) * c)
        v = jnp.concatenate(
            [
                jnp.concatenate([third[0][:, 0:128], third[1][:, 0:128]], axis=1),
                jnp.concatenate([third[0][:, 128:256], third[1][:, 128:256]], axis=1),
            ],
            axis=0,
        )
        scratch[...] = v + dot3((r_hi[...], r_lo[...]), split(v), NN)

        def repack(h, _):
            top8 = sub((8, 128)) < 4
            base = pl.multiple_of(h * 48, 8)
            loaded = [
                [
                    [
                        [scratch[pl.ds(base + 24 * sp + c * count + 8 * i, 8), 128 * b : 128 * b + 128] for i in range(3)]
                        for c in range(2)
                    ]
                    for b in range(2)
                ]
                for sp in range(2)
            ]
            made = []
            for sp in range(2):
                out = [[], []]
                for b in range(2):
                    (a0, a1, a2), (i0, i1, i2) = loaded[sp][b]
                    r1, r2, q1, q2 = sroll(a1), sroll(a2), sroll(i1), sroll(i2)
                    out[0].append((a0, i0, jnp.where(top8, a1, q1)))
                    out[1].append((jnp.where(top8, r1, r2), jnp.where(top8, q1, q2), jnp.where(top8, r2, i2)))
                for k in range(2):
                    (re0, im0, u0), (re1, im1, u1) = out[k]
                    made.append((*dense(re0, re1, im0, im1), *dense_half(u0, u1)))
            for k, t in enumerate(made):
                at = j * owners + 4 * h + k
                for i in range(4):
                    reply_m[at, 8 * i : 8 * i + 8, :] = t[i]
                reply_t[at] = t[4]
            return 0

        lax.fori_loop(0, owners // 4, repack, 0, unroll=2)
        send_chunk(
            j, (0, owners), reply_m, reply_t, back_m, back_t, turned_home, home_of, me_owner,
            s2m.at[j], s2t, r2m, r2t, sa,
        )

    advance(0, range(GATES))
    receive(0)
    advance(1, range(GATES))
    receive(1)
    finish(0)
    finish(1)
    receive(2)
    finish(2)

    @pl.when(at_home)
    def _():
        to_other.wait_send()

    wait_sent(got_w, 0, s1w)
    for j in range(CHUNKS):
        if j == CHUNKS - 1:
            for k in range(GATES):
                gate(j, k)
        wait_sent(sent_t, j * owners, s1t.at[j])

        @pl.when(has_up)
        def _(j=j):
            pltpu.make_async_copy(work.at[j], work.at[j], su.at[j]).wait()

        @pl.when(has_down)
        def _(j=j):
            pltpu.make_async_copy(work.at[j], work.at[j], sd.at[j]).wait()

    for j in range(CHUNKS):
        wait_bytes(back_m, owners, j * owners, r2m.at[j])
        wait_bytes(back_t, owners, j * owners, r2t.at[j])
        wait_sent(reply_m, j * owners, s2m.at[j])
        wait_sent(reply_t, j * owners, s2t.at[j])


def after_kernel(groups, main, tail, pot, ar, ab, out):
    blocks = 3 * groups
    row8 = sub((8, 1))
    decay8, decay4 = jnp.zeros((8, 1), f32), jnp.zeros((8, 1), f32)
    for k in range(8):
        decay8 = jnp.where(row8 == k, ar[k], decay8)
        decay4 = jnp.where(row8 % 4 == k % 4, ar[8 + k % 4], decay4)

    def group(h, _):
        low = lane((8, 128)) < 64
        top = sub((8, 128)) < 4
        made = []
        for g in [2 * h, 2 * h + 1]:
            flat = angle_lanes([jnp.full((8, 128), ab[4 * g + i], f32) for i in range(4)])
            a, b = 2 * g, 2 * g + 1
            ta = [main[a, 8 * i : 8 * i + 8, :] for i in range(4)]
            tb = [main[b, 8 * i : 8 * i + 8, :] for i in range(4)]
            b0, b1, b3 = lroll(tb[0], 64), lroll(tb[1], 64), lroll(tb[3], 64)
            a1, a2 = lroll(ta[1], 64), lroll(ta[2], 64)
            re = (ta[0], jnp.where(low, ta[1], b0), jnp.where(low, b0, b1))
            im = (jnp.where(low, a1, a2), jnp.where(low, a2, tb[1]), tb[2])
            ra, rb = tail_rows(tail[a]), tail_rows(tail[b])
            u = (ta[3], jnp.where(low, ra, b3), jnp.where(low, b3, lroll(rb, 64)))
            for i in range(3):
                k = 3 * g + i
                at = pl.ds(pl.multiple_of(k * 128, 128), 128)
                co, si = phase(0.5 * pot[0:8, at])
                d = jnp.exp(-0.5 * (decay8 + flat[i]))
                co, si = d * co, d * si
                p4 = pot[8:12, at]
                co4, si4 = phase(0.5 * jnp.concatenate([p4, p4], axis=0))
                d = jnp.exp(-0.5 * (decay4 + flat[i]))
                co4, si4 = d * co4, d * si4
                v = co4 * u[i] + jnp.where(top, si4, -si4) * sroll(u[i])
                made.append((k, co * re[i] + si * im[i], co * im[i] - si * re[i], v))
        for k, re, im, v in made:
            out[pl.ds(2 * k, 8, stride=2 * blocks), :] = re
            out[pl.ds(2 * k + 1, 8, stride=2 * blocks), :] = im
            out[pl.ds(16 * blocks + 2 * k, 4, stride=2 * blocks), :] = v[0:4]
            out[pl.ds(16 * blocks + 2 * k + 1, 4, stride=2 * blocks), :] = v[4:8]
        return 0

    lax.fori_loop(0, groups // 2, group, 0, unroll=2)


def body(wave_in, potential, absorb_radial, absorb_bond, coriolis_weight, ladder, angle_step, bond_step, radial_step):
    rows, columns = wave_in.shape[2:]
    blocks = columns // 128
    groups = blocks // 3
    nz = lax.axis_size("sa") // 4
    owners = 4 * nz
    top = lax.axis_size("ka") - 1
    count = radial_step.shape[1]
    full = pl.BlockSpec(memory_space=VMEM)
    smem = pl.BlockSpec(memory_space=pltpu.SMEM)
    hbm = pl.BlockSpec(memory_space=pl.ANY)
    shape = jax.ShapeDtypeStruct
    wave = wave_in.reshape(2, rows, blocks, 128).transpose(1, 2, 0, 3).reshape(rows * blocks * 2, 128)
    pad = jnp.pad(absorb_radial, (0, 128 - rows)).reshape(1, 128)
    weight = jnp.pad(coriolis_weight, (0, 128 - rows)).reshape(1, 128)
    messages = CHUNKS * owners
    main, tail = pl.pallas_call(
        functools.partial(before_kernel, groups),
        out_shape=(shape((messages, 32, 128), f32), shape((messages, 4, 128), f32)),
        in_specs=[full] * 5,
        out_specs=(full, full),
        scratch_shapes=[
            VMEM((rows * (blocks + 1), 128), f32),
            VMEM((121 * groups, 128), f32),
            VMEM((8 * groups, 8 * groups), bf16),
            VMEM((8 * groups, 8 * groups), bf16),
        ],
        compiler_params=pltpu.CompilerParams(vmem_limit_bytes=50 << 20),
        name="before",
    )(wave, potential, pad, absorb_bond.reshape(1, -1), bond_step)
    dma, many = pltpu.SemaphoreType.DMA, pltpu.SemaphoreType.DMA((CHUNKS,))
    back_m, back_t = pl.pallas_call(
        functools.partial(turn_kernel, nz, top),
        out_shape=(shape((messages, 32, 128), f32), shape((messages, 4, 128), f32)),
        in_specs=[hbm, hbm, full, full, full, full],
        out_specs=(hbm, hbm),
        scratch_shapes=[
            VMEM((messages, 32, 128), f32),
            VMEM((messages, 4, 128), f32),
            VMEM((owners, 1, 128), f32),
            VMEM((1, 128), f32),
            VMEM((count, 128), f32),
            VMEM((CHUNKS, 2, count, 256), f32),
            VMEM((CHUNKS, 2, count, 256), f32),
            VMEM((CHUNKS, 2, count, 256), f32),
            VMEM((messages, 32, 128), f32),
            VMEM((messages, 4, 128), f32),
            VMEM((256, 256), bf16),
            VMEM((256, 256), bf16),
            VMEM((256, 256), bf16),
            VMEM((256, 256), bf16),
            VMEM((256, 256), bf16),
            VMEM((256, 256), bf16),
            VMEM((2 * count, 2 * count), bf16),
            VMEM((2 * count, 2 * count), bf16),
            VMEM((2 * count, 256), f32),
            VMEM((1, 2, ANGLES, ANGLES), f32), dma, dma,
            pltpu.SemaphoreType.DMA((CHUNKS, GATES)), many, dma, many, many, dma,
            many, many, many, many,
            many, many, many, many,
        ],
        compiler_params=pltpu.CompilerParams(collective_id=0, has_side_effects=True, vmem_limit_bytes=50 << 20),
        name="turn",
    )(main, tail, weight, angle_step, ladder, radial_step)
    out = pl.pallas_call(
        functools.partial(after_kernel, groups),
        out_shape=shape((rows * blocks * 2, 128), f32),
        in_specs=[full, full, full, smem, smem],
        out_specs=full,
        compiler_params=pltpu.CompilerParams(vmem_limit_bytes=50 << 20),
        name="after",
    )(back_m, back_t, potential, absorb_radial, absorb_bond)
    return out.reshape(rows, blocks, 2, 128).transpose(2, 0, 1, 3).reshape(1, 2, rows, columns)


def solution(mesh):
    return jax.shard_map(
        body,
        mesh=mesh,
        in_specs=(
            P("ka", None, "sa", None),
            P("sa", None),
            P("sa"),
            P(),
            P("sa"),
            P(),
            P("ka", None, None, None),
            P(),
            P(),
        ),
        out_specs=P("ka", None, "sa", None),
        check_vma=False,
    )
```

```python
import functools
import math

import jax
import jax.numpy as jnp
from jax import lax
from jax.experimental import pallas as pl
from jax.experimental.pallas import tpu as pltpu
from jax.sharding import PartitionSpec as P

MESH = pl.DeviceIdType.MESH
VMEM = pltpu.VMEM
CHUNKS = 3
PAIR = 2
ROWS = 12
ANGLES = 96
PACK = 4
GATES = 4
f32, bf16 = jnp.float32, jnp.bfloat16


def split(x):
    high = x.astype(bf16)
    return high, (x - high.astype(f32)).astype(bf16)


def dot3(a, b, dims):
    def one(u, v):
        return lax.dot_general(u, v, (dims, ((), ())), preferred_element_type=f32)

    return one(a[0], b[0]) + (one(a[0], b[1]) + one(a[1], b[0]))


NN = ((1,), (0,))
NT = ((1,), (1,))


def lane(shape):
    return lax.broadcasted_iota(jnp.int32, shape, len(shape) - 1)


def sub(shape):
    return lax.broadcasted_iota(jnp.int32, shape, 0)


def lroll(x, n):
    return pltpu.roll(x, n, 1)


def sroll(x):
    return pltpu.roll(x, 4, 0)


def phase(half):
    s = half * half
    c = 1.0 / 479001600.0
    for k in (-1.0 / 3628800.0, 1.0 / 40320.0, -1.0 / 720.0, 1.0 / 24.0, -0.5, 1.0):
        c = c * s + k
    v = -1.0 / 39916800.0
    for k in (1.0 / 362880.0, -1.0 / 5040.0, 1.0 / 120.0, -1.0 / 6.0, 1.0):
        v = v * s + k
    return c, v * half


def spread(v0, v1, v2):
    n = lane(v0.shape)
    return (
        v0,
        lroll(jnp.where(n >= 96, v0, v1), 32),
        lroll(jnp.where(n >= 64, v1, v2), 64),
        lroll(v2, 96),
    )


def dense(b0, b1, b2, b3):
    n = lane(b0.shape)
    r1, r2, r3 = lroll(b1, 96), lroll(b2, 64), lroll(b3, 32)
    return jnp.where(n < 96, b0, r1), jnp.where(n < 64, r1, r2), jnp.where(n < 32, r2, r3)


def dense_half(u0, u1):
    n = lane(u0.shape)
    r = lroll(u1, 96)
    tail = jnp.where(n < 64, r, sroll(lroll(r, 64)))
    return jnp.where(n < 96, u0, r), tail[0:4]


def tail_rows(tail):
    both = jnp.concatenate([tail, tail], axis=0)
    return jnp.where(sub(both.shape) < 4, both, lroll(both, 64))


def spread_half(tile, tail):
    n = lane(tile.shape)
    return tile, lroll(jnp.where(n >= 96, tile, tail_rows(tail)), 32)


def angle_lanes(values):
    n = lane(values[0].shape[:-1] + (128,))
    a, b, c, d = values
    return jnp.where(n < 96, a, b), jnp.where(n < 64, b, c), jnp.where(n < 32, c, d)


def step_kernel(
    groups, nz, top,
    wave_h, pot_h, ar_h, ab_h, weight_h, angle_h, ladder_h, bond_h, radial_h, out_h,
    wave, pot, ar, ab, weight, angle, ladder, bond, radial,
    pots, bigw, mat, xf, xh, xl, damps, factors, sent_m, sent_t,
    got_m, got_t, got_w, own_w, wide, work, from_up, from_down, reply_m, reply_t, back_m, back_t, outv,
    a_hi, a_lo, u_hi, u_lo, d_hi, d_lo, r_hi, r_lo, scratch,
    angles, in_sems, wave_sems, out_sems, sa_sem, ra_sem,
    s1m, s1t, s1w, r1m, r1t, r1w, su, sd, ru, rd, s2m, s2t, r2m, r2t,
):
    bonds = 4 * groups
    blocks = 3 * groups
    pitch = blocks + 1
    per_row = 2 * blocks
    owners = 4 * nz
    ka, sa = lax.axis_index("ka"), lax.axis_index("sa")
    x, yh = ka // 2, ka % 2
    yl, z, core = sa // (2 * nz), (sa // 2) % nz, sa % 2
    y = 2 * yh + yl
    helicity = 2 * x + core
    me_owner = y * nz + z
    at_home = core == yh

    def owner_of(q, c):
        oy, oz = q // nz, q % nz
        return (2 * x + oy // 2, (oy % 2) * (2 * nz) + oz * 2 + c)

    def home_of(s):
        return (2 * x + core, s)

    def turned(i):
        return ((y + i % 4) % 4) * nz + (z + nz // 2 + i // 4) % nz

    def turned_home(i):
        c, iy, iz = i % 2, (i // 2) % 2, i // 4
        return ((yl + iy) % 2) * (2 * nz) + ((z + nz // 2 + iz) % nz) * 2 + c

    has_up, has_down = helicity < top, helicity > 0
    kx_up = jnp.where(core == 0, x, x + 1)
    kx_down = jnp.where(core == 1, x, x - 1)
    up_dev = (2 * kx_up + yh, yl * (2 * nz) + z * 2 + 1 - core)
    down_dev = (2 * kx_down + yh, yl * (2 * nz) + z * 2 + 1 - core)

    names = ((bond_h, bond), (ab_h, ab), (ar_h, ar), (pot_h, pot), (angle_h, angle), (weight_h, weight))
    names = names + ((ladder_h, ladder), (radial_h, radial))
    loads = [pltpu.make_async_copy(a, b, in_sems.at[k]) for k, (a, b) in enumerate(names)]
    wave_loads = [
        pltpu.make_async_copy(
            wave_h.at[pl.ds(2 * h * per_row, 2 * per_row)], wave.at[pl.ds(2 * h * per_row, 2 * per_row)], wave_sems.at[h]
        )
        for h in range(ROWS // 2)
    ]
    for load in loads[:4] + wave_loads + loads[4:]:
        load.start()

    barrier = pltpu.get_barrier_semaphore()

    def greet(i, _):
        q, s = turned(i), turned_home(i)

        @pl.when(jnp.logical_not(at_home & (q == me_owner)))
        def _():
            pl.semaphore_signal(barrier, inc=1, device_id=owner_of(q, yh), device_id_type=MESH)

        @pl.when(jnp.logical_not(at_home & (s == sa)))
        def _():
            pl.semaphore_signal(barrier, inc=1, device_id=home_of(s), device_id_type=MESH)

        return 0

    lax.fori_loop(0, owners, greet, 0)

    @pl.when(has_up)
    def _():
        pl.semaphore_signal(barrier, inc=1, device_id=up_dev, device_id_type=MESH)

    @pl.when(has_down)
    def _():
        pl.semaphore_signal(barrier, inc=1, device_id=down_dev, device_id_type=MESH)

    for load in loads[:3]:
        load.wait()

    place = lax.broadcasted_iota(jnp.int32, (bonds, bonds), 1)
    point = lax.broadcasted_iota(jnp.int32, (bonds, bonds), 0)
    third_groups = groups // CHUNKS
    wide_rows = 4 * third_groups
    perm = jnp.where(point == 4 * (place % groups) + place // groups, 1.0, 0.0).astype(bf16)
    inside = place % wide_rows
    point_of = 4 * (third_groups * (place // wide_rows) + inside % third_groups) + inside // third_groups
    row_perm = jnp.where(point == point_of, 1.0, 0.0).astype(bf16)
    for c in range(2):
        for k, part in enumerate(split(bond[c])):
            cols = jnp.dot(part, perm, preferred_element_type=f32).astype(bf16)
            rows = lax.dot_general(row_perm, cols, (((0,), (0,)), ((), ())), preferred_element_type=f32)
            rows = rows.astype(bf16)
            for j in range(CHUNKS):
                own = rows[j * wide_rows : (j + 1) * wide_rows]
                at = 2 * k * wide_rows
                if c == 0:
                    mat[j, at : at + wide_rows, 0:bonds] = own
                    mat[j, at + wide_rows : at + 2 * wide_rows, bonds:] = own
                else:
                    mat[j, at : at + wide_rows, bonds:] = -own
                    mat[j, at + wide_rows : at + 2 * wide_rows, 0:bonds] = own

    grid = (groups, bonds)
    cols = []
    for i in range(4):
        mine = jnp.where(lane(grid) == 4 * sub(grid) + i, jnp.broadcast_to(ab[...], grid), 0.0)
        cols.append(jnp.exp(-0.5 * jnp.sum(mine, axis=1, keepdims=True)))
    damp = angle_lanes([jnp.broadcast_to(c, (groups, 128)) for c in cols])
    for i in range(3):
        damps[i] = damp[i]
    decay = jnp.exp(-0.5 * ar[...])

    loads[3].wait()

    def turn(k, _):
        at = pl.ds(pl.multiple_of(k * 128, 128), 128)
        pots[pl.ds(k, 8, stride=pitch), :] = pot[0:8, at]
        pots[pl.ds(8 * pitch + k, 4, stride=pitch), :] = pot[8:12, at]
        return 0

    lax.fori_loop(0, blocks, turn, 0, unroll=4)

    def two_rows(h):
        sides = []
        for k in range(2):
            r = 2 * h + k
            own = jnp.sum(jnp.where(lane((1, ROWS)) == r, decay, 0.0), axis=1, keepdims=True)
            re, im = [], []
            for i in range(3):
                x = wave[pl.ds(r * 2 * blocks + 2 * i, groups, stride=6), :]
                y = wave[pl.ds(r * 2 * blocks + 2 * i + 1, groups, stride=6), :]
                co, si = phase(0.5 * pots[pl.ds(r * pitch + i, groups, stride=3), :])
                d = damp[i] * own
                co, si = d * co, d * si
                re.append(co * x + si * y)
                im.append(co * y - si * x)
            sides.append(jnp.concatenate(spread(*re) + spread(*im), axis=0))
        x = jnp.concatenate(sides, axis=1)
        xf[h] = x
        xh[h], xl[h] = split(x)

    def bond_step(j):
        for h in range(ROWS // 2):
            o = jnp.dot(mat[j], xh[h], preferred_element_type=f32)
            o = o[0 : 2 * wide_rows] + (
                o[2 * wide_rows :] + jnp.dot(mat[j, 0 : 2 * wide_rows], xl[h], preferred_element_type=f32)
            )
            for k in range(2):
                r = 2 * h + k
                for c in range(2):
                    row = r + 8 * c if r < 8 else r + 8 + 4 * c
                    for i in range(4):
                        at = (4 * c + i) * third_groups
                        base = (4 * c + i) * groups + j * third_groups
                        v = o[at : at + third_groups, 128 * k : 128 * k + 128]
                        v = v + xf[h, base : base + third_groups, 128 * k : 128 * k + 128]
                        bigw[pl.ds(i + 5 * row + 121 * j * third_groups, third_groups, stride=121), :] = v

    for h in range(ROWS // 2):
        wave_loads[h].wait()
    for h in range(ROWS // 2):
        two_rows(h)
    bond_step(0)

    def pack(h, _):
        pairs = [PACK * h + k for k in range(PACK)]
        loaded = [
            [bigw[pl.ds(121 * (p // 2) + 2 * (p % 2) + b + 40 * k, 8, stride=5), :] for b in range(2) for k in range(3)]
            for p in pairs
        ]
        made = [
            (*dense(w[0], w[3], w[1], w[4]), *dense_half(w[2], w[5])) for w in loaded
        ]
        for p, t in zip(pairs, made):
            for k in range(4):
                sent_m[p, 8 * k : 8 * k + 8, :] = t[k]
            sent_t[p] = t[4]
        return 0

    batches = owners // PACK
    lax.fori_loop(0, batches, pack, 0, unroll=2)

    expected = 2 * owners - 2 * at_home.astype(jnp.int32)
    expected = expected + has_up.astype(jnp.int32) + has_down.astype(jnp.int32)
    pl.semaphore_wait(barrier, expected)

    def send_chunk(j, part, src_m, src_t, dst_m, dst_t, pick, device, slot, ssm, sst, rsm, rst, self_slot):
        def one(i, _):
            q = pick(i)
            mine = at_home & (q == self_slot)
            here = [
                (src_m.at[j * owners + q], dst_m.at[j * owners + slot], ssm, rsm.at[j]),
                (src_t.at[j * owners + q], dst_t.at[j * owners + slot], sst.at[j], rst.at[j]),
            ]

            @pl.when(mine)
            def _():
                for a, b, _, r in here:
                    pltpu.make_async_copy(a, b, r).start()

            @pl.when(jnp.logical_not(mine))
            def _():
                for a, b, s, r in here:
                    pltpu.make_async_remote_copy(
                        src_ref=a, dst_ref=b, send_sem=s, recv_sem=r, device_id=device(q), device_id_type=MESH
                    ).start()

            return 0

        lax.fori_loop(*part, one, 0)

    def send_weight(i, _):
        q = turned(i)
        mine = at_home & (q == me_owner)

        @pl.when(mine)
        def _():
            pltpu.make_async_copy(own_w, got_w.at[sa], r1w).start()

        @pl.when(jnp.logical_not(mine))
        def _():
            pltpu.make_async_remote_copy(
                src_ref=own_w, dst_ref=got_w.at[sa], send_sem=s1w, recv_sem=r1w,
                device_id=owner_of(q, yh), device_id_type=MESH,
            ).start()

        return 0

    def wait_bytes(ref, count, start, sem):
        view = ref.at[pl.ds(start, count)]
        pltpu.make_async_copy(view, view, sem).wait()

    def wait_sent(ref, start, sem):
        @pl.when(at_home)
        def _():
            wait_bytes(ref, owners - 1, start, sem)

        @pl.when(jnp.logical_not(at_home))
        def _():
            wait_bytes(ref, owners, start, sem)

    size = owners // GATES
    mine_at = (nz // 2) * 4 // size

    def first_send(j, k):
        send_chunk(
            j, (k * size, k * size + size), sent_m, sent_t, got_m, got_t, turned, lambda q: owner_of(q, yh), sa,
            s1m.at[j, k], s1t, r1m, r1t, me_owner,
        )

    def gate(j, k):
        if k != mine_at:
            wait_bytes(sent_m, size, 0, s1m.at[j, k])
        else:

            @pl.when(at_home)
            def _():
                wait_bytes(sent_m, size - 1, 0, s1m.at[j, k])

            @pl.when(jnp.logical_not(at_home))
            def _():
                wait_bytes(sent_m, size, 0, s1m.at[j, k])

    def advance(j, parts):
        for k in parts:
            if j < CHUNKS:
                gate(j, k)
            if j + 1 < CHUNKS:
                first_send(j + 1, k)

    for k in range(GATES):
        first_send(0, k)

    loads[4].wait()
    loads[5].wait()
    own_w[...] = jnp.zeros((1, 128), f32)
    own_w[:, 0:ROWS] = weight[...]
    to_other = pltpu.make_async_remote_copy(
        src_ref=angle, dst_ref=angles, send_sem=sa_sem, recv_sem=ra_sem,
        device_id=(2 * x + 1 - yh, sa), device_id_type=MESH,
    )

    @pl.when(at_home)
    def _():
        to_other.start()
        angles[...] = angle[...]

    lax.fori_loop(0, owners, send_weight, 0)
    for j in range(1, CHUNKS):
        bond_step(j)
        lax.fori_loop(j * batches, (j + 1) * batches, pack, 0, unroll=2)
    loads[6].wait()
    loads[7].wait()

    def fill(parts, hi, lo, shape):
        scratch[0 : shape[0], 0 : shape[1]] = jnp.zeros(shape, f32)
        for row, col, value in parts:
            scratch[row : row + ANGLES, col : col + ANGLES] = value
        high, low = split(scratch[0 : shape[0], 0 : shape[1]])
        hi[...] = high
        lo[...] = low

    coef_up, coef_down = 0.0, 0.0
    for k in range(top + 1):
        coef_up = jnp.where(helicity == k, math.sqrt(top * (top + 1) - k * (k + 1)), coef_up)
        coef_down = jnp.where(helicity == k, math.sqrt(top * (top + 1) - (k - 1) * k), coef_down)
    up = coef_up * ladder[...]
    down = coef_down * ladder[...]
    fill([(0, 128, up), (128, 0, -up)], u_hi, u_lo, (256, 256))
    fill([(128, 0, down), (0, 128, -down)], d_hi, d_lo, (256, 256))
    count = radial.shape[1]
    for c in range(2):
        high, low = split(radial[c])
        for part, mat in ((high, r_hi), (low, r_lo)):
            if c == 0:
                mat[0:count, 0:count] = part
                mat[count:, count:] = part
            else:
                mat[0:count, count:] = -part
                mat[count:, 0:count] = part

    for buf, has in ((from_up, has_up), (from_down, has_down)):

        @pl.when(jnp.logical_not(has))
        def _(buf=buf):
            buf[...] = jnp.zeros(buf.shape, f32)

    def column(row_of):
        shape = (8, ROWS)
        mine = jnp.where(lane(shape) == row_of(sub(shape)), jnp.broadcast_to(decay, shape), 0.0)
        return jnp.sum(mine, axis=1, keepdims=True)

    decay8, decay4 = column(lambda n: n), column(lambda n: 8 + n % 4)

    def make_factor(g, _):
        top4 = sub((8, 128)) < 4
        made = []
        for i in range(3):
            at = pl.ds(pl.multiple_of((3 * g + i) * 128, 128), 128)
            flat = damps[i, pl.ds(g, 1), :]
            p4 = pot[8:12, at]
            for half, own in ((pot[0:8, at], decay8), (jnp.concatenate([p4, p4], axis=0), decay4)):
                co, si = phase(0.5 * half)
                d = own * flat
                made.append((at, d * co, d * si))
        for n, (at, co, si) in enumerate(made):
            if n % 2:
                si = jnp.where(top4, si, -si)
            factors[2 * (n % 2), :, at] = co
            factors[2 * (n % 2) + 1, :, at] = si
        return 0

    lax.fori_loop(0, groups, make_factor, 0, unroll=2)

    @pl.when(jnp.logical_not(at_home))
    def _():
        to_other.wait_recv()

    fill(
        [(0, 0, angles[0, 0]), (128, 128, angles[0, 0]), (0, 128, -angles[0, 1]), (128, 0, angles[0, 1])],
        a_hi, a_lo, (256, 256),
    )
    wait_bytes(got_w, owners, 0, r1w)

    def weights(sp, _):
        shape = (2 * ROWS, 128)
        row = sub(shape)
        a = jnp.where(row < ROWS, got_w[2 * sp], got_w[2 * sp + 1])
        a = jnp.where(lane(shape) == jnp.where(row < ROWS, row, row - ROWS), a, 0.0)
        at = pl.ds(pl.multiple_of(sp * 2 * ROWS, 8), 2 * ROWS)
        wide[at, :] = jnp.broadcast_to(jnp.sum(a, axis=1, keepdims=True), shape)
        return 0

    lax.fori_loop(0, owners // 2, weights, 0)

    def receive(j):
        wait_bytes(got_m, owners, j * owners, r1m.at[j])
        wait_bytes(got_t, owners, j * owners, r1t.at[j])

        def unpack(h, _):
            top8 = sub((8, 128)) < 4
            loaded = [
                [got_m[j * owners + 4 * h + k, 8 * i : 8 * i + 8, :] for i in range(4)] + [got_t[j * owners + 4 * h + k]]
                for k in range(4)
            ]
            got = []
            for t in loaded:
                re0, re1, im0, im1 = spread(t[0], t[1], t[2])
                u0, u1 = spread_half(t[3], t[4])
                got.append(((re0, im0, u0), (re1, im1, u1)))
            made = []
            for sp in range(2):
                for b in range(2):
                    (re_a, im_a, u_a), (re_b, im_b, u_b) = got[2 * sp][b], got[2 * sp + 1][b]
                    re_b, im_b = sroll(re_b), sroll(im_b)
                    tiles = (
                        (re_a, jnp.where(top8, u_a, re_b), jnp.where(top8, re_b, sroll(u_b))),
                        (im_a, jnp.where(top8, sroll(u_a), im_b), jnp.where(top8, im_b, u_b)),
                    )
                    made += [(24 * sp + 8 * i, b, c, tiles[c][i]) for c in range(2) for i in range(3)]
            base = pl.multiple_of(h * 48, 8)
            for at, b, c, tile in made:
                work[j, b, pl.ds(base + at, 8), 128 * c : 128 * c + 128] = tile
            return 0

        lax.fori_loop(0, owners // 4, unpack, 0, unroll=2)
        for b in range(2):
            v = work[j, b]
            work[j, b] = v + dot3(split(v), (a_hi[...], a_lo[...]), NT)

        @pl.when(has_up)
        def _():
            pltpu.make_async_remote_copy(
                src_ref=work.at[j], dst_ref=from_down.at[j], send_sem=su.at[j], recv_sem=rd.at[j],
                device_id=up_dev, device_id_type=MESH,
            ).start()

        @pl.when(has_down)
        def _():
            pltpu.make_async_remote_copy(
                src_ref=work.at[j], dst_ref=from_up.at[j], send_sem=sd.at[j], recv_sem=ru.at[j],
                device_id=down_dev, device_id_type=MESH,
            ).start()


    def finish(j):
        @pl.when(has_up)
        def _():
            pltpu.make_async_copy(from_up.at[j], from_up.at[j], ru.at[j]).wait()

        @pl.when(has_down)
        def _():
            pltpu.make_async_copy(from_down.at[j], from_down.at[j], rd.at[j]).wait()

        third = []
        for b in range(2):
            c = dot3(split(from_up[j, b]), (u_hi[...], u_lo[...]), NT)
            c = c + dot3(split(from_down[j, b]), (d_hi[...], d_lo[...]), NN)
            w = wide[...]
            third.append(work[j, b] + jnp.concatenate([w, w], axis=1) * c)
        v = jnp.concatenate(
            [
                jnp.concatenate([third[0][:, 0:128], third[1][:, 0:128]], axis=1),
                jnp.concatenate([third[0][:, 128:256], third[1][:, 128:256]], axis=1),
            ],
            axis=0,
        )
        scratch[...] = v + dot3((r_hi[...], r_lo[...]), split(v), NN)

        def repack(h, _):
            top8 = sub((8, 128)) < 4
            base = pl.multiple_of(h * 48, 8)
            loaded = [
                [
                    [
                        [scratch[pl.ds(base + 24 * sp + c * count + 8 * i, 8), 128 * b : 128 * b + 128] for i in range(3)]
                        for c in range(2)
                    ]
                    for b in range(2)
                ]
                for sp in range(2)
            ]
            made = []
            for sp in range(2):
                out = [[], []]
                for b in range(2):
                    (a0, a1, a2), (i0, i1, i2) = loaded[sp][b]
                    r1, r2, q1, q2 = sroll(a1), sroll(a2), sroll(i1), sroll(i2)
                    out[0].append((a0, i0, jnp.where(top8, a1, q1)))
                    out[1].append((jnp.where(top8, r1, r2), jnp.where(top8, q1, q2), jnp.where(top8, r2, i2)))
                for k in range(2):
                    (re0, im0, u0), (re1, im1, u1) = out[k]
                    made.append((*dense(re0, re1, im0, im1), *dense_half(u0, u1)))
            for k, t in enumerate(made):
                at = j * owners + 4 * h + k
                for i in range(4):
                    reply_m[at, 8 * i : 8 * i + 8, :] = t[i]
                reply_t[at] = t[4]
            return 0

        lax.fori_loop(0, owners // 4, repack, 0, unroll=2)
        send_chunk(
            j, (0, owners), reply_m, reply_t, back_m, back_t, turned_home, home_of, me_owner,
            s2m.at[j], s2t, r2m, r2t, sa,
        )

    def leave(j):
        wait_bytes(back_m, owners, j * owners, r2m.at[j])
        wait_bytes(back_t, owners, j * owners, r2t.at[j])

        def group(h, _):
            low = lane((8, 128)) < 64
            made = []
            for g in [2 * h, 2 * h + 1]:
                a, b = 2 * g, 2 * g + 1
                ta = [back_m[a, 8 * i : 8 * i + 8, :] for i in range(4)]
                tb = [back_m[b, 8 * i : 8 * i + 8, :] for i in range(4)]
                b0, b1, b3 = lroll(tb[0], 64), lroll(tb[1], 64), lroll(tb[3], 64)
                a1, a2 = lroll(ta[1], 64), lroll(ta[2], 64)
                re = (ta[0], jnp.where(low, ta[1], b0), jnp.where(low, b0, b1))
                im = (jnp.where(low, a1, a2), jnp.where(low, a2, tb[1]), tb[2])
                ra, rb = tail_rows(back_t[a]), tail_rows(back_t[b])
                u = (ta[3], jnp.where(low, ra, b3), jnp.where(low, b3, lroll(rb, 64)))
                for i in range(3):
                    k = 3 * g + i
                    at = pl.ds(pl.multiple_of(k * 128, 128), 128)
                    co, si, co4, si4 = [factors[n, :, at] for n in range(4)]
                    v = co4 * u[i] + si4 * sroll(u[i])
                    made.append((k, co * re[i] + si * im[i], co * im[i] - si * re[i], v))
            for k, re, im, v in made:
                outv[pl.ds(2 * k, 8, stride=per_row), :] = re
                outv[pl.ds(2 * k + 1, 8, stride=per_row), :] = im
                outv[pl.ds(8 * per_row + 2 * k, 4, stride=per_row), :] = v[0:4]
                outv[pl.ds(8 * per_row + 2 * k + 1, 4, stride=per_row), :] = v[4:8]
            return 0

        part = groups // CHUNKS // 2
        lax.fori_loop(j * part, (j + 1) * part, group, 0, unroll=2)
        width = per_row // CHUNKS

        def store(r, _):
            at = pl.ds(pl.multiple_of(r * per_row + j * width, 8), width)
            pltpu.make_async_copy(outv.at[at], out_h.at[at], out_sems.at[j]).start()
            return 0

        lax.fori_loop(0, ROWS, store, 0)

    advance(0, range(GATES))
    receive(0)
    advance(1, range(GATES))
    receive(1)
    finish(0)
    finish(1)
    receive(2)
    finish(2)
    for j in range(CHUNKS):
        leave(j)

    @pl.when(at_home)
    def _():
        to_other.wait_send()

    wait_sent(got_w, 0, s1w)
    for j in range(CHUNKS):
        if j == CHUNKS - 1:
            for k in range(GATES):
                gate(j, k)
        wait_sent(sent_t, j * owners, s1t.at[j])

        @pl.when(has_up)
        def _(j=j):
            pltpu.make_async_copy(work.at[j], work.at[j], su.at[j]).wait()

        @pl.when(has_down)
        def _(j=j):
            pltpu.make_async_copy(work.at[j], work.at[j], sd.at[j]).wait()

    for j in range(CHUNKS):
        wait_sent(reply_m, j * owners, s2m.at[j])
        wait_sent(reply_t, j * owners, s2t.at[j])
        whole = pl.ds(0, ROWS * per_row // CHUNKS)
        pltpu.make_async_copy(outv.at[whole], out_h.at[whole], out_sems.at[j]).wait()


def body(wave_in, potential, absorb_radial, absorb_bond, coriolis_weight, ladder, angle_step, bond_step, radial_step):
    rows, columns = wave_in.shape[2:]
    blocks = columns // 128
    groups = blocks // 3
    bonds = 4 * groups
    nz = lax.axis_size("sa") // 4
    owners = 4 * nz
    top = lax.axis_size("ka") - 1
    count = radial_step.shape[1]
    hbm = pl.BlockSpec(memory_space=pl.ANY)
    wave = wave_in.reshape(2, rows, blocks, 128).transpose(1, 2, 0, 3).reshape(rows * blocks * 2, 128)
    messages = CHUNKS * owners
    dma, many = pltpu.SemaphoreType.DMA, pltpu.SemaphoreType.DMA((CHUNKS,))
    small = VMEM((256, 256), bf16)
    out = pl.pallas_call(
        functools.partial(step_kernel, groups, nz, top),
        out_shape=jax.ShapeDtypeStruct((rows * blocks * 2, 128), f32),
        in_specs=[hbm] * 9,
        out_specs=hbm,
        scratch_shapes=[
            VMEM((rows * blocks * 2, 128), f32),
            VMEM((rows, columns), f32),
            VMEM((1, rows), f32),
            VMEM((1, bonds), f32),
            VMEM((1, rows), f32),
            VMEM((1, 2, ANGLES, ANGLES), f32),
            VMEM((ANGLES, ANGLES), f32),
            VMEM((2, bonds, bonds), f32),
            VMEM((2, count, count), f32),
            VMEM((rows * (blocks + 1), 128), f32),
            VMEM((121 * groups, 128), f32),
            VMEM((CHUNKS, 4 * bonds // CHUNKS, 2 * bonds), bf16),
            VMEM((rows // 2, 2 * bonds, 256), f32),
            VMEM((rows // 2, 2 * bonds, 256), bf16),
            VMEM((rows // 2, 2 * bonds, 256), bf16),
            VMEM((3, groups, 128), f32),
            VMEM((4, 8, columns), f32),
            VMEM((messages, 32, 128), f32),
            VMEM((messages, 4, 128), f32),
            VMEM((messages, 32, 128), f32),
            VMEM((messages, 4, 128), f32),
            VMEM((owners, 1, 128), f32),
            VMEM((1, 128), f32),
            VMEM((count, 128), f32),
            VMEM((CHUNKS, 2, count, 256), f32),
            VMEM((CHUNKS, 2, count, 256), f32),
            VMEM((CHUNKS, 2, count, 256), f32),
            VMEM((messages, 32, 128), f32),
            VMEM((messages, 4, 128), f32),
            VMEM((messages, 32, 128), f32),
            VMEM((messages, 4, 128), f32),
            VMEM((rows * blocks * 2, 128), f32),
            small, small, small, small, small, small,
            VMEM((2 * count, 2 * count), bf16),
            VMEM((2 * count, 2 * count), bf16),
            VMEM((2 * count, 256), f32),
            VMEM((1, 2, ANGLES, ANGLES), f32),
            pltpu.SemaphoreType.DMA((8,)), pltpu.SemaphoreType.DMA((rows // 2,)), many, dma, dma,
            pltpu.SemaphoreType.DMA((CHUNKS, GATES)), many, dma, many, many, dma,
            many, many, many, many,
            many, many, many, many,
        ],
        compiler_params=pltpu.CompilerParams(collective_id=0, has_side_effects=True, vmem_limit_bytes=58 << 20),
        name="step",
    )(
        wave, potential, absorb_radial.reshape(1, -1), absorb_bond.reshape(1, -1), coriolis_weight.reshape(1, -1),
        angle_step, ladder, bond_step, radial_step,
    )
    return out.reshape(rows, blocks, 2, 128).transpose(2, 0, 1, 3).reshape(1, 2, rows, columns)


def solution(mesh):
    return jax.shard_map(
        body,
        mesh=mesh,
        in_specs=(
            P("ka", None, "sa", None),
            P("sa", None),
            P("sa"),
            P(),
            P("sa"),
            P(),
            P("ka", None, None, None),
            P(),
            P(),
        ),
        out_specs=P("ka", None, "sa", None),
        check_vma=False,
    )
```

```python
import functools
import math

import jax
import jax.numpy as jnp
from jax import lax
from jax.experimental import pallas as pl
from jax.experimental.pallas import tpu as pltpu
from jax.sharding import PartitionSpec as P

MESH = pl.DeviceIdType.MESH
VMEM = pltpu.VMEM
CHUNKS = 3
PAIR = 2
ROWS = 12
ANGLES = 96
PACK = 4
GATES = 4
ORDER = (2, 1, 3, 0)
f32, bf16 = jnp.float32, jnp.bfloat16


def split(x):
    high = x.astype(bf16)
    return high, (x - high.astype(f32)).astype(bf16)


def dot3(a, b, dims):
    def one(u, v):
        return lax.dot_general(u, v, (dims, ((), ())), preferred_element_type=f32)

    return one(a[0], b[0]) + (one(a[0], b[1]) + one(a[1], b[0]))


NN = ((1,), (0,))
NT = ((1,), (1,))


def lane(shape):
    return lax.broadcasted_iota(jnp.int32, shape, len(shape) - 1)


def sub(shape):
    return lax.broadcasted_iota(jnp.int32, shape, 0)


def lroll(x, n):
    return pltpu.roll(x, n, 1)


def sroll(x):
    return pltpu.roll(x, 4, 0)


def phase(half):
    s = half * half
    c = 1.0 / 479001600.0
    for k in (-1.0 / 3628800.0, 1.0 / 40320.0, -1.0 / 720.0, 1.0 / 24.0, -0.5, 1.0):
        c = c * s + k
    v = -1.0 / 39916800.0
    for k in (1.0 / 362880.0, -1.0 / 5040.0, 1.0 / 120.0, -1.0 / 6.0, 1.0):
        v = v * s + k
    return c, v * half


def spread(v0, v1, v2):
    n = lane(v0.shape)
    return (
        v0,
        lroll(jnp.where(n >= 96, v0, v1), 32),
        lroll(jnp.where(n >= 64, v1, v2), 64),
        lroll(v2, 96),
    )


def dense(b0, b1, b2, b3):
    n = lane(b0.shape)
    r1, r2, r3 = lroll(b1, 96), lroll(b2, 64), lroll(b3, 32)
    return jnp.where(n < 96, b0, r1), jnp.where(n < 64, r1, r2), jnp.where(n < 32, r2, r3)


def dense_half(u0, u1):
    n = lane(u0.shape)
    r = lroll(u1, 96)
    tail = jnp.where(n < 64, r, sroll(lroll(r, 64)))
    return jnp.where(n < 96, u0, r), tail[0:4]


def tail_rows(tail):
    both = jnp.concatenate([tail, tail], axis=0)
    return jnp.where(sub(both.shape) < 4, both, lroll(both, 64))


def spread_half(tile, tail):
    n = lane(tile.shape)
    return tile, lroll(jnp.where(n >= 96, tile, tail_rows(tail)), 32)


def angle_lanes(values):
    n = lane(values[0].shape[:-1] + (128,))
    a, b, c, d = values
    return jnp.where(n < 96, a, b), jnp.where(n < 64, b, c), jnp.where(n < 32, c, d)


def step_kernel(
    groups, nz, top,
    wave_h, pot_h, ar_h, ab_h, weight_h, angle_h, ladder_h, bond_h, radial_h, out_h,
    wave, pot, ar, ab, weight, angle, ladder, bond, radial,
    pots, bigw, mat, xf, xh, xl, damps, factors, sent_m, sent_t,
    got_m, got_t, got_w, own_w, wide, work, from_up, from_down, reply_m, reply_t, back_m, back_t, outv,
    a_hi, a_lo, u_hi, u_lo, d_hi, d_lo, r_hi, r_lo, scratch,
    angles, in_sems, wave_sems, out_sems, sa_sem, ra_sem,
    s1m, s1t, s1w, r1m, r1t, r1w, su, sd, ru, rd, s2m, s2t, r2m, r2t,
):
    bonds = 4 * groups
    blocks = 3 * groups
    pitch = blocks + 1
    per_row = 2 * blocks
    owners = 4 * nz
    ka, sa = lax.axis_index("ka"), lax.axis_index("sa")
    x, yh = ka // 2, ka % 2
    yl, z, core = sa // (2 * nz), (sa // 2) % nz, sa % 2
    y = 2 * yh + yl
    helicity = 2 * x + core
    me_owner = y * nz + z
    at_home = core == yh

    def owner_of(q, c):
        oy, oz = q // nz, q % nz
        return (2 * x + oy // 2, (oy % 2) * (2 * nz) + oz * 2 + c)

    def home_of(s):
        return (2 * x + core, s)

    def turned(i):
        return ((y + i % 4) % 4) * nz + (z + nz // 2 + i // 4) % nz

    def turned_home(i):
        c, iy, iz = i % 2, (i // 2) % 2, i // 4
        return ((yl + iy) % 2) * (2 * nz) + ((z + nz // 2 + iz) % nz) * 2 + c

    def early_home(i):
        c, iy, iz = i % 2, (i // 2) % 2, i // 4
        first = 3
        away = jnp.where(iz < first, iz, first + (z + nz // 2 + iz) % (nz - first))
        return ((yl + iy) % 2) * (2 * nz) + away * 2 + c

    has_up, has_down = helicity < top, helicity > 0
    kx_up = jnp.where(core == 0, x, x + 1)
    kx_down = jnp.where(core == 1, x, x - 1)
    up_dev = (2 * kx_up + yh, yl * (2 * nz) + z * 2 + 1 - core)
    down_dev = (2 * kx_down + yh, yl * (2 * nz) + z * 2 + 1 - core)

    names = ((bond_h, bond), (ab_h, ab), (ar_h, ar), (pot_h, pot), (angle_h, angle), (weight_h, weight))
    names = names + ((ladder_h, ladder), (radial_h, radial))
    loads = [pltpu.make_async_copy(a, b, in_sems.at[k]) for k, (a, b) in enumerate(names)]
    wave_loads = [
        pltpu.make_async_copy(
            wave_h.at[pl.ds(2 * h * per_row, 2 * per_row)], wave.at[pl.ds(2 * h * per_row, 2 * per_row)], wave_sems.at[h]
        )
        for h in range(ROWS // 2)
    ]
    for load in loads[:4] + wave_loads:
        load.start()

    barrier = pltpu.get_barrier_semaphore()

    def greet(i, _):
        q, s = turned(i), turned_home(i)

        @pl.when(jnp.logical_not(at_home & (q == me_owner)))
        def _():
            pl.semaphore_signal(barrier, inc=1, device_id=owner_of(q, yh), device_id_type=MESH)

        @pl.when(jnp.logical_not(at_home & (s == sa)))
        def _():
            pl.semaphore_signal(barrier, inc=1, device_id=home_of(s), device_id_type=MESH)

        return 0

    lax.fori_loop(0, owners, greet, 0)

    @pl.when(has_up)
    def _():
        pl.semaphore_signal(barrier, inc=1, device_id=up_dev, device_id_type=MESH)

    @pl.when(has_down)
    def _():
        pl.semaphore_signal(barrier, inc=1, device_id=down_dev, device_id_type=MESH)

    for load in loads[:3]:
        load.wait()

    place = lax.broadcasted_iota(jnp.int32, (bonds, bonds), 1)
    point = lax.broadcasted_iota(jnp.int32, (bonds, bonds), 0)
    third_groups = groups // CHUNKS
    wide_rows = 4 * third_groups
    perm = jnp.where(point == 4 * (place % groups) + place // groups, 1.0, 0.0).astype(bf16)
    inside = place % wide_rows
    point_of = 4 * (third_groups * (place // wide_rows) + inside % third_groups) + inside // third_groups
    row_perm = jnp.where(point == point_of, 1.0, 0.0).astype(bf16)
    for c in range(2):
        for k, part in enumerate(split(bond[c])):
            cols = jnp.dot(part, perm, preferred_element_type=f32).astype(bf16)
            rows = lax.dot_general(row_perm, cols, (((0,), (0,)), ((), ())), preferred_element_type=f32)
            rows = rows.astype(bf16)
            for j in range(CHUNKS):
                own = rows[j * wide_rows : (j + 1) * wide_rows]
                at = 2 * k * wide_rows
                if c == 0:
                    mat[j, at : at + wide_rows, 0:bonds] = own
                    mat[j, at + wide_rows : at + 2 * wide_rows, bonds:] = own
                else:
                    mat[j, at : at + wide_rows, bonds:] = -own
                    mat[j, at + wide_rows : at + 2 * wide_rows, 0:bonds] = own

    grid = (groups, bonds)
    cols = []
    for i in range(4):
        mine = jnp.where(lane(grid) == 4 * sub(grid) + i, jnp.broadcast_to(ab[...], grid), 0.0)
        cols.append(jnp.exp(-0.5 * jnp.sum(mine, axis=1, keepdims=True)))
    damp = angle_lanes([jnp.broadcast_to(c, (groups, 128)) for c in cols])
    for i in range(3):
        damps[i] = damp[i]
    decay = jnp.exp(-0.5 * ar[...])

    loads[3].wait()

    def turn(k, _):
        at = pl.ds(pl.multiple_of(k * 128, 128), 128)
        pots[pl.ds(k, 8, stride=pitch), :] = pot[0:8, at]
        pots[pl.ds(8 * pitch + k, 4, stride=pitch), :] = pot[8:12, at]
        return 0

    lax.fori_loop(0, blocks, turn, 0, unroll=4)

    def two_rows(h):
        sides = []
        for k in range(2):
            r = 2 * h + k
            own = jnp.sum(jnp.where(lane((1, ROWS)) == r, decay, 0.0), axis=1, keepdims=True)
            re, im = [], []
            for i in range(3):
                x = wave[pl.ds(r * 2 * blocks + 2 * i, groups, stride=6), :]
                y = wave[pl.ds(r * 2 * blocks + 2 * i + 1, groups, stride=6), :]
                co, si = phase(0.5 * pots[pl.ds(r * pitch + i, groups, stride=3), :])
                d = damp[i] * own
                co, si = d * co, d * si
                re.append(co * x + si * y)
                im.append(co * y - si * x)
            sides.append(jnp.concatenate(spread(*re) + spread(*im), axis=0))
        x = jnp.concatenate(sides, axis=1)
        xf[h] = x
        xh[h], xl[h] = split(x)

    def bond_step(j):
        for h in range(ROWS // 2):
            o = jnp.dot(mat[j], xh[h], preferred_element_type=f32)
            o = o[0 : 2 * wide_rows] + (
                o[2 * wide_rows :] + jnp.dot(mat[j, 0 : 2 * wide_rows], xl[h], preferred_element_type=f32)
            )
            for k in range(2):
                r = 2 * h + k
                for c in range(2):
                    row = r + 8 * c if r < 8 else r + 8 + 4 * c
                    for i in range(4):
                        at = (4 * c + i) * third_groups
                        base = (4 * c + i) * groups + j * third_groups
                        v = o[at : at + third_groups, 128 * k : 128 * k + 128]
                        v = v + xf[h, base : base + third_groups, 128 * k : 128 * k + 128]
                        bigw[pl.ds(i + 5 * row + 121 * j * third_groups, third_groups, stride=121), :] = v

    for h in range(ROWS // 2):
        wave_loads[h].wait()
    for load in loads[4:]:
        load.start()
    for h in range(ROWS // 2):
        two_rows(h)
    bond_step(0)

    def pack(h, _):
        pairs = [PACK * h + k for k in range(PACK)]
        loaded = [
            [bigw[pl.ds(121 * (p // 2) + 2 * (p % 2) + b + 40 * k, 8, stride=5), :] for b in range(2) for k in range(3)]
            for p in pairs
        ]
        made = [
            (*dense(w[0], w[3], w[1], w[4]), *dense_half(w[2], w[5])) for w in loaded
        ]
        for p, t in zip(pairs, made):
            for k in range(4):
                sent_m[p, 8 * k : 8 * k + 8, :] = t[k]
            sent_t[p] = t[4]
        return 0

    batches = owners // PACK
    lax.fori_loop(0, batches, pack, 0, unroll=2)

    expected = 2 * owners - 2 * at_home.astype(jnp.int32)
    expected = expected + has_up.astype(jnp.int32) + has_down.astype(jnp.int32)
    pl.semaphore_wait(barrier, expected)

    def send_chunk(j, part, src_m, src_t, dst_m, dst_t, pick, device, slot, ssm, sst, rsm, rst, self_slot):
        def one(i, _):
            q = pick(i)
            mine = at_home & (q == self_slot)
            here = [
                (src_m.at[j * owners + q], dst_m.at[j * owners + slot], ssm, rsm.at[j]),
                (src_t.at[j * owners + q], dst_t.at[j * owners + slot], sst.at[j], rst.at[j]),
            ]

            @pl.when(mine)
            def _():
                for a, b, _, r in here:
                    pltpu.make_async_copy(a, b, r).start()

            @pl.when(jnp.logical_not(mine))
            def _():
                for a, b, s, r in here:
                    pltpu.make_async_remote_copy(
                        src_ref=a, dst_ref=b, send_sem=s, recv_sem=r, device_id=device(q), device_id_type=MESH
                    ).start()

            return 0

        lax.fori_loop(*part, one, 0)

    def send_weight(i, _):
        q = turned(i)
        mine = at_home & (q == me_owner)

        @pl.when(mine)
        def _():
            pltpu.make_async_copy(own_w, got_w.at[sa], r1w).start()

        @pl.when(jnp.logical_not(mine))
        def _():
            pltpu.make_async_remote_copy(
                src_ref=own_w, dst_ref=got_w.at[sa], send_sem=s1w, recv_sem=r1w,
                device_id=owner_of(q, yh), device_id_type=MESH,
            ).start()

        return 0

    def wait_bytes(ref, count, start, sem):
        view = ref.at[pl.ds(start, count)]
        pltpu.make_async_copy(view, view, sem).wait()

    def wait_sent(ref, start, sem):
        @pl.when(at_home)
        def _():
            wait_bytes(ref, owners - 1, start, sem)

        @pl.when(jnp.logical_not(at_home))
        def _():
            wait_bytes(ref, owners, start, sem)

    size = owners // GATES
    mine_at = (nz // 2) * 4 // size

    def first_send(j, k):
        send_chunk(
            j, (k * size, k * size + size), sent_m, sent_t, got_m, got_t, turned, lambda q: owner_of(q, yh), sa,
            s1m.at[j, k], s1t, r1m, r1t, me_owner,
        )

    def gate(j, k):
        if k != mine_at:
            wait_bytes(sent_m, size, 0, s1m.at[j, k])
        else:

            @pl.when(at_home)
            def _():
                wait_bytes(sent_m, size - 1, 0, s1m.at[j, k])

            @pl.when(jnp.logical_not(at_home))
            def _():
                wait_bytes(sent_m, size, 0, s1m.at[j, k])

    def advance(j):
        for k in ORDER:
            if j < CHUNKS:
                gate(j, k)
            if j + 1 < CHUNKS:
                first_send(j + 1, k)

    for k in range(GATES):
        first_send(0, k)

    loads[4].wait()
    loads[5].wait()
    own_w[...] = jnp.zeros((1, 128), f32)
    own_w[:, 0:ROWS] = weight[...]
    to_other = pltpu.make_async_remote_copy(
        src_ref=angle, dst_ref=angles, send_sem=sa_sem, recv_sem=ra_sem,
        device_id=(2 * x + 1 - yh, sa), device_id_type=MESH,
    )

    @pl.when(at_home)
    def _():
        to_other.start()
        angles[...] = angle[...]

    lax.fori_loop(0, owners, send_weight, 0)
    for j in range(1, CHUNKS):
        bond_step(j)
        lax.fori_loop(j * batches, (j + 1) * batches, pack, 0, unroll=2)
    loads[6].wait()
    loads[7].wait()

    def fill(parts, hi, lo, shape):
        scratch[0 : shape[0], 0 : shape[1]] = jnp.zeros(shape, f32)
        for row, col, value in parts:
            scratch[row : row + ANGLES, col : col + ANGLES] = value
        high, low = split(scratch[0 : shape[0], 0 : shape[1]])
        hi[...] = high
        lo[...] = low

    coef_up, coef_down = 0.0, 0.0
    for k in range(top + 1):
        coef_up = jnp.where(helicity == k, math.sqrt(top * (top + 1) - k * (k + 1)), coef_up)
        coef_down = jnp.where(helicity == k, math.sqrt(top * (top + 1) - (k - 1) * k), coef_down)
    up = coef_up * ladder[...]
    down = coef_down * ladder[...]
    fill([(0, 128, up), (128, 0, -up)], u_hi, u_lo, (256, 256))
    fill([(128, 0, down), (0, 128, -down)], d_hi, d_lo, (256, 256))
    count = radial.shape[1]
    for c in range(2):
        high, low = split(radial[c])
        for part, mat in ((high, r_hi), (low, r_lo)):
            if c == 0:
                mat[0:count, 0:count] = part
                mat[count:, count:] = part
            else:
                mat[0:count, count:] = -part
                mat[count:, 0:count] = part

    for buf, has in ((from_up, has_up), (from_down, has_down)):

        @pl.when(jnp.logical_not(has))
        def _(buf=buf):
            buf[...] = jnp.zeros(buf.shape, f32)

    def column(row_of):
        shape = (8, ROWS)
        mine = jnp.where(lane(shape) == row_of(sub(shape)), jnp.broadcast_to(decay, shape), 0.0)
        return jnp.sum(mine, axis=1, keepdims=True)

    decay8, decay4 = column(lambda n: n), column(lambda n: 8 + n % 4)

    def make_factor(g, _):
        top4 = sub((8, 128)) < 4
        made = []
        for i in range(3):
            at = pl.ds(pl.multiple_of((3 * g + i) * 128, 128), 128)
            flat = damps[i, pl.ds(g, 1), :]
            p4 = pot[8:12, at]
            for half, own in ((pot[0:8, at], decay8), (jnp.concatenate([p4, p4], axis=0), decay4)):
                co, si = phase(0.5 * half)
                d = own * flat
                made.append((at, d * co, d * si))
        for n, (at, co, si) in enumerate(made):
            if n % 2:
                si = jnp.where(top4, si, -si)
            factors[2 * (n % 2), :, at] = co
            factors[2 * (n % 2) + 1, :, at] = si
        return 0

    lax.fori_loop(0, groups, make_factor, 0, unroll=2)

    @pl.when(jnp.logical_not(at_home))
    def _():
        to_other.wait_recv()

    fill(
        [(0, 0, angles[0, 0]), (128, 128, angles[0, 0]), (0, 128, -angles[0, 1]), (128, 0, angles[0, 1])],
        a_hi, a_lo, (256, 256),
    )
    wait_bytes(got_w, owners, 0, r1w)

    def weights(sp, _):
        shape = (2 * ROWS, 128)
        row = sub(shape)
        a = jnp.where(row < ROWS, got_w[2 * sp], got_w[2 * sp + 1])
        a = jnp.where(lane(shape) == jnp.where(row < ROWS, row, row - ROWS), a, 0.0)
        at = pl.ds(pl.multiple_of(sp * 2 * ROWS, 8), 2 * ROWS)
        wide[at, :] = jnp.broadcast_to(jnp.sum(a, axis=1, keepdims=True), shape)
        return 0

    lax.fori_loop(0, owners // 2, weights, 0)

    def receive(j):
        wait_bytes(got_m, owners, j * owners, r1m.at[j])
        wait_bytes(got_t, owners, j * owners, r1t.at[j])

        def unpack(h, _):
            top8 = sub((8, 128)) < 4
            loaded = [
                [got_m[j * owners + 4 * h + k, 8 * i : 8 * i + 8, :] for i in range(4)] + [got_t[j * owners + 4 * h + k]]
                for k in range(4)
            ]
            got = []
            for t in loaded:
                re0, re1, im0, im1 = spread(t[0], t[1], t[2])
                u0, u1 = spread_half(t[3], t[4])
                got.append(((re0, im0, u0), (re1, im1, u1)))
            made = []
            for sp in range(2):
                for b in range(2):
                    (re_a, im_a, u_a), (re_b, im_b, u_b) = got[2 * sp][b], got[2 * sp + 1][b]
                    re_b, im_b = sroll(re_b), sroll(im_b)
                    tiles = (
                        (re_a, jnp.where(top8, u_a, re_b), jnp.where(top8, re_b, sroll(u_b))),
                        (im_a, jnp.where(top8, sroll(u_a), im_b), jnp.where(top8, im_b, u_b)),
                    )
                    made += [(24 * sp + 8 * i, b, c, tiles[c][i]) for c in range(2) for i in range(3)]
            base = pl.multiple_of(h * 48, 8)
            for at, b, c, tile in made:
                work[j, b, pl.ds(base + at, 8), 128 * c : 128 * c + 128] = tile
            return 0

        lax.fori_loop(0, owners // 4, unpack, 0, unroll=2)
        for b in range(2):
            v = work[j, b]
            work[j, b] = v + dot3(split(v), (a_hi[...], a_lo[...]), NT)

        @pl.when(has_up)
        def _():
            pltpu.make_async_remote_copy(
                src_ref=work.at[j], dst_ref=from_down.at[j], send_sem=su.at[j], recv_sem=rd.at[j],
                device_id=up_dev, device_id_type=MESH,
            ).start()

        @pl.when(has_down)
        def _():
            pltpu.make_async_remote_copy(
                src_ref=work.at[j], dst_ref=from_up.at[j], send_sem=sd.at[j], recv_sem=ru.at[j],
                device_id=down_dev, device_id_type=MESH,
            ).start()


    def finish(j):
        @pl.when(has_up)
        def _():
            pltpu.make_async_copy(from_up.at[j], from_up.at[j], ru.at[j]).wait()

        @pl.when(has_down)
        def _():
            pltpu.make_async_copy(from_down.at[j], from_down.at[j], rd.at[j]).wait()

        third = []
        for b in range(2):
            c = dot3(split(from_up[j, b]), (u_hi[...], u_lo[...]), NT)
            c = c + dot3(split(from_down[j, b]), (d_hi[...], d_lo[...]), NN)
            w = wide[...]
            third.append(work[j, b] + jnp.concatenate([w, w], axis=1) * c)
        v = jnp.concatenate(
            [
                jnp.concatenate([third[0][:, 0:128], third[1][:, 0:128]], axis=1),
                jnp.concatenate([third[0][:, 128:256], third[1][:, 128:256]], axis=1),
            ],
            axis=0,
        )
        scratch[...] = v + dot3((r_hi[...], r_lo[...]), split(v), NN)

        def repack(h, _):
            top8 = sub((8, 128)) < 4
            base = pl.multiple_of(h * 48, 8)
            loaded = [
                [
                    [
                        [scratch[pl.ds(base + 24 * sp + c * count + 8 * i, 8), 128 * b : 128 * b + 128] for i in range(3)]
                        for c in range(2)
                    ]
                    for b in range(2)
                ]
                for sp in range(2)
            ]
            made = []
            for sp in range(2):
                out = [[], []]
                for b in range(2):
                    (a0, a1, a2), (i0, i1, i2) = loaded[sp][b]
                    r1, r2, q1, q2 = sroll(a1), sroll(a2), sroll(i1), sroll(i2)
                    out[0].append((a0, i0, jnp.where(top8, a1, q1)))
                    out[1].append((jnp.where(top8, r1, r2), jnp.where(top8, q1, q2), jnp.where(top8, r2, i2)))
                for k in range(2):
                    (re0, im0, u0), (re1, im1, u1) = out[k]
                    made.append((*dense(re0, re1, im0, im1), *dense_half(u0, u1)))
            for k, t in enumerate(made):
                at = j * owners + 4 * h + k
                for i in range(4):
                    reply_m[at, 8 * i : 8 * i + 8, :] = t[i]
                reply_t[at] = t[4]
            return 0

        lax.fori_loop(0, owners // 4, repack, 0, unroll=2)

    def reply(j, k):
        send_chunk(
            j, (k * size, k * size + size), reply_m, reply_t, back_m, back_t, early_home, home_of, me_owner,
            s2m.at[j], s2t, r2m, r2t, sa,
        )

    def leave(j):
        wait_bytes(back_m, owners, j * owners, r2m.at[j])
        wait_bytes(back_t, owners, j * owners, r2t.at[j])

        def group(h, _):
            low = lane((8, 128)) < 64
            made = []
            for g in [2 * h, 2 * h + 1]:
                a, b = 2 * g, 2 * g + 1
                ta = [back_m[a, 8 * i : 8 * i + 8, :] for i in range(4)]
                tb = [back_m[b, 8 * i : 8 * i + 8, :] for i in range(4)]
                b0, b1, b3 = lroll(tb[0], 64), lroll(tb[1], 64), lroll(tb[3], 64)
                a1, a2 = lroll(ta[1], 64), lroll(ta[2], 64)
                re = (ta[0], jnp.where(low, ta[1], b0), jnp.where(low, b0, b1))
                im = (jnp.where(low, a1, a2), jnp.where(low, a2, tb[1]), tb[2])
                ra, rb = tail_rows(back_t[a]), tail_rows(back_t[b])
                u = (ta[3], jnp.where(low, ra, b3), jnp.where(low, b3, lroll(rb, 64)))
                for i in range(3):
                    k = 3 * g + i
                    at = pl.ds(pl.multiple_of(k * 128, 128), 128)
                    co, si, co4, si4 = [factors[n, :, at] for n in range(4)]
                    v = co4 * u[i] + si4 * sroll(u[i])
                    made.append((k, co * re[i] + si * im[i], co * im[i] - si * re[i], v))
            for k, re, im, v in made:
                outv[pl.ds(2 * k, 8, stride=per_row), :] = re
                outv[pl.ds(2 * k + 1, 8, stride=per_row), :] = im
                outv[pl.ds(8 * per_row + 2 * k, 4, stride=per_row), :] = v[0:4]
                outv[pl.ds(8 * per_row + 2 * k + 1, 4, stride=per_row), :] = v[4:8]
            return 0

        part = groups // CHUNKS // 2
        lax.fori_loop(j * part, (j + 1) * part, group, 0, unroll=2)
        width = per_row // CHUNKS

        def store(r, _):
            at = pl.ds(pl.multiple_of(r * per_row + j * width, 8), width)
            pltpu.make_async_copy(outv.at[at], out_h.at[at], out_sems.at[j]).start()
            return 0

        lax.fori_loop(0, ROWS, store, 0)

    advance(0)
    receive(0)
    advance(1)
    receive(1)
    finish(0)
    for k in ORDER:
        gate(2, k)
        reply(0, k)
    receive(2)
    finish(1)
    for k in range(GATES):
        reply(1, k)
    finish(2)
    for k in range(GATES):
        reply(2, k)
    for j in range(CHUNKS):
        leave(j)

    @pl.when(at_home)
    def _():
        to_other.wait_send()

    wait_sent(got_w, 0, s1w)
    for j in range(CHUNKS):
        wait_sent(sent_t, j * owners, s1t.at[j])

        @pl.when(has_up)
        def _(j=j):
            pltpu.make_async_copy(work.at[j], work.at[j], su.at[j]).wait()

        @pl.when(has_down)
        def _(j=j):
            pltpu.make_async_copy(work.at[j], work.at[j], sd.at[j]).wait()

    for j in range(CHUNKS):
        wait_sent(reply_m, j * owners, s2m.at[j])
        wait_sent(reply_t, j * owners, s2t.at[j])
        whole = pl.ds(0, ROWS * per_row // CHUNKS)
        pltpu.make_async_copy(outv.at[whole], out_h.at[whole], out_sems.at[j]).wait()


def body(wave_in, potential, absorb_radial, absorb_bond, coriolis_weight, ladder, angle_step, bond_step, radial_step):
    rows, columns = wave_in.shape[2:]
    blocks = columns // 128
    groups = blocks // 3
    bonds = 4 * groups
    nz = lax.axis_size("sa") // 4
    owners = 4 * nz
    top = lax.axis_size("ka") - 1
    count = radial_step.shape[1]
    hbm = pl.BlockSpec(memory_space=pl.ANY)
    wave = wave_in.reshape(2, rows, blocks, 128).transpose(1, 2, 0, 3).reshape(rows * blocks * 2, 128)
    messages = CHUNKS * owners
    dma, many = pltpu.SemaphoreType.DMA, pltpu.SemaphoreType.DMA((CHUNKS,))
    small = VMEM((256, 256), bf16)
    out = pl.pallas_call(
        functools.partial(step_kernel, groups, nz, top),
        out_shape=jax.ShapeDtypeStruct((rows * blocks * 2, 128), f32),
        in_specs=[hbm] * 9,
        out_specs=hbm,
        scratch_shapes=[
            VMEM((rows * blocks * 2, 128), f32),
            VMEM((rows, columns), f32),
            VMEM((1, rows), f32),
            VMEM((1, bonds), f32),
            VMEM((1, rows), f32),
            VMEM((1, 2, ANGLES, ANGLES), f32),
            VMEM((ANGLES, ANGLES), f32),
            VMEM((2, bonds, bonds), f32),
            VMEM((2, count, count), f32),
            VMEM((rows * (blocks + 1), 128), f32),
            VMEM((121 * groups, 128), f32),
            VMEM((CHUNKS, 4 * bonds // CHUNKS, 2 * bonds), bf16),
            VMEM((rows // 2, 2 * bonds, 256), f32),
            VMEM((rows // 2, 2 * bonds, 256), bf16),
            VMEM((rows // 2, 2 * bonds, 256), bf16),
            VMEM((3, groups, 128), f32),
            VMEM((4, 8, columns), f32),
            VMEM((messages, 32, 128), f32),
            VMEM((messages, 4, 128), f32),
            VMEM((messages, 32, 128), f32),
            VMEM((messages, 4, 128), f32),
            VMEM((owners, 1, 128), f32),
            VMEM((1, 128), f32),
            VMEM((count, 128), f32),
            VMEM((CHUNKS, 2, count, 256), f32),
            VMEM((CHUNKS, 2, count, 256), f32),
            VMEM((CHUNKS, 2, count, 256), f32),
            VMEM((messages, 32, 128), f32),
            VMEM((messages, 4, 128), f32),
            VMEM((messages, 32, 128), f32),
            VMEM((messages, 4, 128), f32),
            VMEM((rows * blocks * 2, 128), f32),
            small, small, small, small, small, small,
            VMEM((2 * count, 2 * count), bf16),
            VMEM((2 * count, 2 * count), bf16),
            VMEM((2 * count, 256), f32),
            VMEM((1, 2, ANGLES, ANGLES), f32),
            pltpu.SemaphoreType.DMA((8,)), pltpu.SemaphoreType.DMA((rows // 2,)), many, dma, dma,
            pltpu.SemaphoreType.DMA((CHUNKS, GATES)), many, dma, many, many, dma,
            many, many, many, many,
            many, many, many, many,
        ],
        compiler_params=pltpu.CompilerParams(collective_id=0, has_side_effects=True, vmem_limit_bytes=58 << 20),
        name="step",
    )(
        wave, potential, absorb_radial.reshape(1, -1), absorb_bond.reshape(1, -1), coriolis_weight.reshape(1, -1),
        angle_step, ladder, bond_step, radial_step,
    )
    return out.reshape(rows, blocks, 2, 128).transpose(2, 0, 1, 3).reshape(1, 2, rows, columns)


def solution(mesh):
    return jax.shard_map(
        body,
        mesh=mesh,
        in_specs=(
            P("ka", None, "sa", None),
            P("sa", None),
            P("sa"),
            P(),
            P("sa"),
            P(),
            P("ka", None, None, None),
            P(),
            P(),
        ),
        out_specs=P("ka", None, "sa", None),
        check_vma=False,
    )
```

```python
import functools
import math

import jax
import jax.numpy as jnp
from jax import lax
from jax.experimental import pallas as pl
from jax.experimental.pallas import tpu as pltpu
from jax.sharding import PartitionSpec as P

MESH = pl.DeviceIdType.MESH
VMEM = pltpu.VMEM
CHUNKS = 3
PAIR = 2
ROWS = 12
ANGLES = 96
PACK = 4
GATES = 4
ORDER = (2, 1, 3, 0)
f32, bf16 = jnp.float32, jnp.bfloat16


def split(x):
    high = x.astype(bf16)
    return high, (x - high.astype(f32)).astype(bf16)


def dot3(a, b, dims):
    def one(u, v):
        return lax.dot_general(u, v, (dims, ((), ())), preferred_element_type=f32)

    return one(a[0], b[0]) + (one(a[0], b[1]) + one(a[1], b[0]))


NN = ((1,), (0,))
NT = ((1,), (1,))


def lane(shape):
    return lax.broadcasted_iota(jnp.int32, shape, len(shape) - 1)


def sub(shape):
    return lax.broadcasted_iota(jnp.int32, shape, 0)


def lroll(x, n):
    return pltpu.roll(x, n, 1)


def sroll(x):
    return pltpu.roll(x, 4, 0)


def phase(half):
    s = half * half
    c = 1.0 / 479001600.0
    for k in (-1.0 / 3628800.0, 1.0 / 40320.0, -1.0 / 720.0, 1.0 / 24.0, -0.5, 1.0):
        c = c * s + k
    v = -1.0 / 39916800.0
    for k in (1.0 / 362880.0, -1.0 / 5040.0, 1.0 / 120.0, -1.0 / 6.0, 1.0):
        v = v * s + k
    return c, v * half


def spread(v0, v1, v2):
    n = lane(v0.shape)
    return (
        v0,
        lroll(jnp.where(n >= 96, v0, v1), 32),
        lroll(jnp.where(n >= 64, v1, v2), 64),
        lroll(v2, 96),
    )


def dense(b0, b1, b2, b3):
    n = lane(b0.shape)
    r1, r2, r3 = lroll(b1, 96), lroll(b2, 64), lroll(b3, 32)
    return jnp.where(n < 96, b0, r1), jnp.where(n < 64, r1, r2), jnp.where(n < 32, r2, r3)


def dense_half(u0, u1):
    n = lane(u0.shape)
    r = lroll(u1, 96)
    tail = jnp.where(n < 64, r, sroll(lroll(r, 64)))
    return jnp.where(n < 96, u0, r), tail[0:4]


def tail_rows(tail):
    both = jnp.concatenate([tail, tail], axis=0)
    return jnp.where(sub(both.shape) < 4, both, lroll(both, 64))


def spread_half(tile, tail):
    n = lane(tile.shape)
    return tile, lroll(jnp.where(n >= 96, tile, tail_rows(tail)), 32)


def angle_lanes(values):
    n = lane(values[0].shape[:-1] + (128,))
    a, b, c, d = values
    return jnp.where(n < 96, a, b), jnp.where(n < 64, b, c), jnp.where(n < 32, c, d)


def step_kernel(
    groups, nz, top,
    wave_h, pot_h, ar_h, ab_h, weight_h, angle_h, ladder_h, bond_h, radial_h, out_h,
    wave, pot, ar, ab, weight, angle, ladder, bond, radial,
    pots, bigw, mat, xf, xh, xl, damps, factors, sent_m, sent_t,
    got_m, got_t, got_w, own_w, wide, work, from_up, from_down, reply_m, reply_t, back_m, back_t, outv,
    a_hi, a_lo, u_hi, u_lo, d_hi, d_lo, r_hi, r_lo, scratch,
    angles, in_sems, wave_sems, out_sems, sa_sem, ra_sem,
    s1m, s1t, s1w, r1m, r1t, r1w, su, sd, ru, rd, s2m, s2t, r2m, r2t,
):
    bonds = 4 * groups
    blocks = 3 * groups
    pitch = blocks + 1
    per_row = 2 * blocks
    owners = 4 * nz
    ka, sa = lax.axis_index("ka"), lax.axis_index("sa")
    x, yh = ka // 2, ka % 2
    yl, z, core = sa // (2 * nz), (sa // 2) % nz, sa % 2
    y = 2 * yh + yl
    helicity = 2 * x + core
    me_owner = y * nz + z
    at_home = core == yh

    def owner_of(q, c):
        oy, oz = q // nz, q % nz
        return (2 * x + oy // 2, (oy % 2) * (2 * nz) + oz * 2 + c)

    def home_of(s):
        return (2 * x + core, s)

    def turned(i):
        return ((y + i % 4) % 4) * nz + (z + nz // 2 + i // 4) % nz

    def turned_home(i):
        c, iy, iz = i % 2, (i // 2) % 2, i // 4
        return ((yl + iy) % 2) * (2 * nz) + ((z + nz // 2 + iz) % nz) * 2 + c

    def early_home(i):
        c, iy, iz = i % 2, (i // 2) % 2, i // 4
        first = 3
        away = jnp.where(iz < first, iz, first + (z + nz // 2 + iz) % (nz - first))
        return ((yl + iy) % 2) * (2 * nz) + away * 2 + c

    has_up, has_down = helicity < top, helicity > 0
    kx_up = jnp.where(core == 0, x, x + 1)
    kx_down = jnp.where(core == 1, x, x - 1)
    up_dev = (2 * kx_up + yh, yl * (2 * nz) + z * 2 + 1 - core)
    down_dev = (2 * kx_down + yh, yl * (2 * nz) + z * 2 + 1 - core)

    names = ((bond_h, bond), (ab_h, ab), (ar_h, ar), (pot_h, pot), (angle_h, angle), (weight_h, weight))
    names = names + ((ladder_h, ladder), (radial_h, radial))
    loads = [pltpu.make_async_copy(a, b, in_sems.at[k]) for k, (a, b) in enumerate(names)]
    wave_loads = [
        pltpu.make_async_copy(
            wave_h.at[pl.ds(2 * h * per_row, 2 * per_row)], wave.at[pl.ds(2 * h * per_row, 2 * per_row)], wave_sems.at[h]
        )
        for h in range(ROWS // 2)
    ]
    for load in loads[:4] + wave_loads:
        load.start()

    barrier = pltpu.get_barrier_semaphore()

    def greet(i, _):
        q, s = turned(i), turned_home(i)

        @pl.when(jnp.logical_not(at_home & (q == me_owner)))
        def _():
            pl.semaphore_signal(barrier, inc=1, device_id=owner_of(q, yh), device_id_type=MESH)

        @pl.when(jnp.logical_not(at_home & (s == sa)))
        def _():
            pl.semaphore_signal(barrier, inc=1, device_id=home_of(s), device_id_type=MESH)

        return 0

    lax.fori_loop(0, owners, greet, 0)

    @pl.when(has_up)
    def _():
        pl.semaphore_signal(barrier, inc=1, device_id=up_dev, device_id_type=MESH)

    @pl.when(has_down)
    def _():
        pl.semaphore_signal(barrier, inc=1, device_id=down_dev, device_id_type=MESH)

    for load in loads[:3]:
        load.wait()

    place = lax.broadcasted_iota(jnp.int32, (bonds, bonds), 1)
    point = lax.broadcasted_iota(jnp.int32, (bonds, bonds), 0)
    third_groups = groups // CHUNKS
    wide_rows = 4 * third_groups
    perm = jnp.where(point == 4 * (place % groups) + place // groups, 1.0, 0.0).astype(bf16)
    inside = place % wide_rows
    point_of = 4 * (third_groups * (place // wide_rows) + inside % third_groups) + inside // third_groups
    row_perm = jnp.where(point == point_of, 1.0, 0.0).astype(bf16)
    for c in range(2):
        for k, part in enumerate(split(bond[c])):
            cols = jnp.dot(part, perm, preferred_element_type=f32).astype(bf16)
            rows = lax.dot_general(row_perm, cols, (((0,), (0,)), ((), ())), preferred_element_type=f32)
            rows = rows.astype(bf16)
            for j in range(CHUNKS):
                own = rows[j * wide_rows : (j + 1) * wide_rows]
                at = 2 * k * wide_rows
                if c == 0:
                    mat[j, at : at + wide_rows, 0:bonds] = own
                    mat[j, at + wide_rows : at + 2 * wide_rows, bonds:] = own
                else:
                    mat[j, at : at + wide_rows, bonds:] = -own
                    mat[j, at + wide_rows : at + 2 * wide_rows, 0:bonds] = own

    grid = (groups, bonds)
    cols = []
    for i in range(4):
        mine = jnp.where(lane(grid) == 4 * sub(grid) + i, jnp.broadcast_to(ab[...], grid), 0.0)
        cols.append(jnp.exp(-0.5 * jnp.sum(mine, axis=1, keepdims=True)))
    damp = angle_lanes([jnp.broadcast_to(c, (groups, 128)) for c in cols])
    for i in range(3):
        damps[i] = damp[i]
    decay = jnp.exp(-0.5 * ar[...])

    loads[3].wait()

    def turn(k, _):
        at = pl.ds(pl.multiple_of(k * 128, 128), 128)
        pots[pl.ds(k, 8, stride=pitch), :] = pot[0:8, at]
        pots[pl.ds(8 * pitch + k, 4, stride=pitch), :] = pot[8:12, at]
        return 0

    lax.fori_loop(0, blocks, turn, 0, unroll=4)

    def two_rows(h):
        sides = []
        for k in range(2):
            r = 2 * h + k
            own = jnp.sum(jnp.where(lane((1, ROWS)) == r, decay, 0.0), axis=1, keepdims=True)
            re, im = [], []
            for i in range(3):
                x = wave[pl.ds(r * 2 * blocks + 2 * i, groups, stride=6), :]
                y = wave[pl.ds(r * 2 * blocks + 2 * i + 1, groups, stride=6), :]
                co, si = phase(0.5 * pots[pl.ds(r * pitch + i, groups, stride=3), :])
                d = damp[i] * own
                co, si = d * co, d * si
                re.append(co * x + si * y)
                im.append(co * y - si * x)
            sides.append(jnp.concatenate(spread(*re) + spread(*im), axis=0))
        x = jnp.concatenate(sides, axis=1)
        xf[h] = x
        xh[h], xl[h] = split(x)

    def bond_step(j):
        for h in range(ROWS // 2):
            o = jnp.dot(mat[j], xh[h], preferred_element_type=f32)
            o = o[0 : 2 * wide_rows] + (
                o[2 * wide_rows :] + jnp.dot(mat[j, 0 : 2 * wide_rows], xl[h], preferred_element_type=f32)
            )
            for k in range(2):
                r = 2 * h + k
                for c in range(2):
                    row = r + 8 * c if r < 8 else r + 8 + 4 * c
                    for i in range(4):
                        at = (4 * c + i) * third_groups
                        base = (4 * c + i) * groups + j * third_groups
                        v = o[at : at + third_groups, 128 * k : 128 * k + 128]
                        v = v + xf[h, base : base + third_groups, 128 * k : 128 * k + 128]
                        bigw[pl.ds(i + 5 * row + 121 * j * third_groups, third_groups, stride=121), :] = v

    for h in range(ROWS // 2):
        wave_loads[h].wait()
    for load in loads[4:]:
        load.start()
    for h in range(ROWS // 2):
        two_rows(h)
    bond_step(0)

    def pack_all(pairs):
        loaded = [
            [bigw[pl.ds(121 * (p // 2) + 2 * (p % 2) + b + 40 * k, 8, stride=5), :] for b in range(2) for k in range(3)]
            for p in pairs
        ]
        made = [
            (*dense(w[0], w[3], w[1], w[4]), *dense_half(w[2], w[5])) for w in loaded
        ]
        for p, t in zip(pairs, made):
            for k in range(4):
                sent_m[p, 8 * k : 8 * k + 8, :] = t[k]
            sent_t[p] = t[4]

    def pack(h, _):
        pack_all([PACK * h + k for k in range(PACK)])
        return 0

    batches = owners // PACK

    expected = 2 * owners - 2 * at_home.astype(jnp.int32)
    expected = expected + has_up.astype(jnp.int32) + has_down.astype(jnp.int32)
    pl.semaphore_wait(barrier, expected)

    def send_chunk(j, part, src_m, src_t, dst_m, dst_t, pick, device, slot, ssm, sst, rsm, rst, self_slot):
        def one(i, _):
            q = pick(i)
            mine = at_home & (q == self_slot)
            here = [
                (src_m.at[j * owners + q], dst_m.at[j * owners + slot], ssm, rsm.at[j]),
                (src_t.at[j * owners + q], dst_t.at[j * owners + slot], sst.at[j], rst.at[j]),
            ]

            @pl.when(mine)
            def _():
                for a, b, _, r in here:
                    pltpu.make_async_copy(a, b, r).start()

            @pl.when(jnp.logical_not(mine))
            def _():
                for a, b, s, r in here:
                    pltpu.make_async_remote_copy(
                        src_ref=a, dst_ref=b, send_sem=s, recv_sem=r, device_id=device(q), device_id_type=MESH
                    ).start()

            return 0

        lax.fori_loop(*part, one, 0)

    def send_weight(i, _):
        q = turned(i)
        mine = at_home & (q == me_owner)

        @pl.when(mine)
        def _():
            pltpu.make_async_copy(own_w, got_w.at[sa], r1w).start()

        @pl.when(jnp.logical_not(mine))
        def _():
            pltpu.make_async_remote_copy(
                src_ref=own_w, dst_ref=got_w.at[sa], send_sem=s1w, recv_sem=r1w,
                device_id=owner_of(q, yh), device_id_type=MESH,
            ).start()

        return 0

    def wait_bytes(ref, count, start, sem):
        view = ref.at[pl.ds(start, count)]
        pltpu.make_async_copy(view, view, sem).wait()

    def wait_sent(ref, start, sem):
        @pl.when(at_home)
        def _():
            wait_bytes(ref, owners - 1, start, sem)

        @pl.when(jnp.logical_not(at_home))
        def _():
            wait_bytes(ref, owners, start, sem)

    size = owners // GATES
    mine_at = (nz // 2) * 4 // size

    def first_send(j, k):
        send_chunk(
            j, (k * size, k * size + size), sent_m, sent_t, got_m, got_t, turned, lambda q: owner_of(q, yh), sa,
            s1m.at[j, k], s1t, r1m, r1t, me_owner,
        )

    def gate(j, k):
        if k != mine_at:
            wait_bytes(sent_m, size, 0, s1m.at[j, k])
        else:

            @pl.when(at_home)
            def _():
                wait_bytes(sent_m, size - 1, 0, s1m.at[j, k])

            @pl.when(jnp.logical_not(at_home))
            def _():
                wait_bytes(sent_m, size, 0, s1m.at[j, k])

    def advance(j):
        for k in ORDER:
            if j < CHUNKS:
                gate(j, k)
            if j + 1 < CHUNKS:
                first_send(j + 1, k)

    for k in range(GATES):
        for i in range(nz // GATES):
            plane = (z + nz // 2 + k * (nz // GATES) + i) % nz
            pack_all([iy * nz + plane for iy in range(4)])
        first_send(0, k)

    loads[4].wait()
    loads[5].wait()
    own_w[...] = jnp.zeros((1, 128), f32)
    own_w[:, 0:ROWS] = weight[...]
    to_other = pltpu.make_async_remote_copy(
        src_ref=angle, dst_ref=angles, send_sem=sa_sem, recv_sem=ra_sem,
        device_id=(2 * x + 1 - yh, sa), device_id_type=MESH,
    )

    @pl.when(at_home)
    def _():
        to_other.start()
        angles[...] = angle[...]

    lax.fori_loop(0, owners, send_weight, 0)
    for j in range(1, CHUNKS):
        bond_step(j)
        lax.fori_loop(j * batches, (j + 1) * batches, pack, 0, unroll=2)
    loads[6].wait()
    loads[7].wait()

    def fill(parts, hi, lo, shape):
        scratch[0 : shape[0], 0 : shape[1]] = jnp.zeros(shape, f32)
        for row, col, value in parts:
            scratch[row : row + ANGLES, col : col + ANGLES] = value
        high, low = split(scratch[0 : shape[0], 0 : shape[1]])
        hi[...] = high
        lo[...] = low

    coef_up, coef_down = 0.0, 0.0
    for k in range(top + 1):
        coef_up = jnp.where(helicity == k, math.sqrt(top * (top + 1) - k * (k + 1)), coef_up)
        coef_down = jnp.where(helicity == k, math.sqrt(top * (top + 1) - (k - 1) * k), coef_down)
    up = coef_up * ladder[...]
    down = coef_down * ladder[...]
    fill([(0, 128, up), (128, 0, -up)], u_hi, u_lo, (256, 256))
    fill([(128, 0, down), (0, 128, -down)], d_hi, d_lo, (256, 256))
    count = radial.shape[1]
    for c in range(2):
        high, low = split(radial[c])
        for part, mat in ((high, r_hi), (low, r_lo)):
            if c == 0:
                mat[0:count, 0:count] = part
                mat[count:, count:] = part
            else:
                mat[0:count, count:] = -part
                mat[count:, 0:count] = part

    for buf, has in ((from_up, has_up), (from_down, has_down)):

        @pl.when(jnp.logical_not(has))
        def _(buf=buf):
            buf[...] = jnp.zeros(buf.shape, f32)

    def column(row_of):
        shape = (8, ROWS)
        mine = jnp.where(lane(shape) == row_of(sub(shape)), jnp.broadcast_to(decay, shape), 0.0)
        return jnp.sum(mine, axis=1, keepdims=True)

    decay8, decay4 = column(lambda n: n), column(lambda n: 8 + n % 4)

    def make_factor(g, _):
        top4 = sub((8, 128)) < 4
        made = []
        for i in range(3):
            at = pl.ds(pl.multiple_of((3 * g + i) * 128, 128), 128)
            flat = damps[i, pl.ds(g, 1), :]
            p4 = pot[8:12, at]
            for half, own in ((pot[0:8, at], decay8), (jnp.concatenate([p4, p4], axis=0), decay4)):
                co, si = phase(0.5 * half)
                d = own * flat
                made.append((at, d * co, d * si))
        for n, (at, co, si) in enumerate(made):
            if n % 2:
                si = jnp.where(top4, si, -si)
            factors[2 * (n % 2), :, at] = co
            factors[2 * (n % 2) + 1, :, at] = si
        return 0

    lax.fori_loop(0, groups, make_factor, 0, unroll=2)

    @pl.when(jnp.logical_not(at_home))
    def _():
        to_other.wait_recv()

    fill(
        [(0, 0, angles[0, 0]), (128, 128, angles[0, 0]), (0, 128, -angles[0, 1]), (128, 0, angles[0, 1])],
        a_hi, a_lo, (256, 256),
    )
    wait_bytes(got_w, owners, 0, r1w)

    def weights(sp, _):
        shape = (2 * ROWS, 128)
        row = sub(shape)
        a = jnp.where(row < ROWS, got_w[2 * sp], got_w[2 * sp + 1])
        a = jnp.where(lane(shape) == jnp.where(row < ROWS, row, row - ROWS), a, 0.0)
        at = pl.ds(pl.multiple_of(sp * 2 * ROWS, 8), 2 * ROWS)
        wide[at, :] = jnp.broadcast_to(jnp.sum(a, axis=1, keepdims=True), shape)
        return 0

    lax.fori_loop(0, owners // 2, weights, 0)

    def receive(j):
        wait_bytes(got_m, owners, j * owners, r1m.at[j])
        wait_bytes(got_t, owners, j * owners, r1t.at[j])

        def unpack(h, _):
            top8 = sub((8, 128)) < 4
            loaded = [
                [got_m[j * owners + 4 * h + k, 8 * i : 8 * i + 8, :] for i in range(4)] + [got_t[j * owners + 4 * h + k]]
                for k in range(4)
            ]
            got = []
            for t in loaded:
                re0, re1, im0, im1 = spread(t[0], t[1], t[2])
                u0, u1 = spread_half(t[3], t[4])
                got.append(((re0, im0, u0), (re1, im1, u1)))
            made = []
            for sp in range(2):
                for b in range(2):
                    (re_a, im_a, u_a), (re_b, im_b, u_b) = got[2 * sp][b], got[2 * sp + 1][b]
                    re_b, im_b = sroll(re_b), sroll(im_b)
                    tiles = (
                        (re_a, jnp.where(top8, u_a, re_b), jnp.where(top8, re_b, sroll(u_b))),
                        (im_a, jnp.where(top8, sroll(u_a), im_b), jnp.where(top8, im_b, u_b)),
                    )
                    made += [(24 * sp + 8 * i, b, c, tiles[c][i]) for c in range(2) for i in range(3)]
            base = pl.multiple_of(h * 48, 8)
            for at, b, c, tile in made:
                work[j, b, pl.ds(base + at, 8), 128 * c : 128 * c + 128] = tile
            return 0

        lax.fori_loop(0, owners // 4, unpack, 0, unroll=2)
        for b in range(2):
            v = work[j, b]
            work[j, b] = v + dot3(split(v), (a_hi[...], a_lo[...]), NT)

        @pl.when(has_up)
        def _():
            pltpu.make_async_remote_copy(
                src_ref=work.at[j], dst_ref=from_down.at[j], send_sem=su.at[j], recv_sem=rd.at[j],
                device_id=up_dev, device_id_type=MESH,
            ).start()

        @pl.when(has_down)
        def _():
            pltpu.make_async_remote_copy(
                src_ref=work.at[j], dst_ref=from_up.at[j], send_sem=sd.at[j], recv_sem=ru.at[j],
                device_id=down_dev, device_id_type=MESH,
            ).start()


    def finish(j):
        @pl.when(has_up)
        def _():
            pltpu.make_async_copy(from_up.at[j], from_up.at[j], ru.at[j]).wait()

        @pl.when(has_down)
        def _():
            pltpu.make_async_copy(from_down.at[j], from_down.at[j], rd.at[j]).wait()

        third = []
        for b in range(2):
            c = dot3(split(from_up[j, b]), (u_hi[...], u_lo[...]), NT)
            c = c + dot3(split(from_down[j, b]), (d_hi[...], d_lo[...]), NN)
            w = wide[...]
            third.append(work[j, b] + jnp.concatenate([w, w], axis=1) * c)
        v = jnp.concatenate(
            [
                jnp.concatenate([third[0][:, 0:128], third[1][:, 0:128]], axis=1),
                jnp.concatenate([third[0][:, 128:256], third[1][:, 128:256]], axis=1),
            ],
            axis=0,
        )
        scratch[...] = v + dot3((r_hi[...], r_lo[...]), split(v), NN)

        def repack(h, _):
            top8 = sub((8, 128)) < 4
            base = pl.multiple_of(h * 48, 8)
            loaded = [
                [
                    [
                        [scratch[pl.ds(base + 24 * sp + c * count + 8 * i, 8), 128 * b : 128 * b + 128] for i in range(3)]
                        for c in range(2)
                    ]
                    for b in range(2)
                ]
                for sp in range(2)
            ]
            made = []
            for sp in range(2):
                out = [[], []]
                for b in range(2):
                    (a0, a1, a2), (i0, i1, i2) = loaded[sp][b]
                    r1, r2, q1, q2 = sroll(a1), sroll(a2), sroll(i1), sroll(i2)
                    out[0].append((a0, i0, jnp.where(top8, a1, q1)))
                    out[1].append((jnp.where(top8, r1, r2), jnp.where(top8, q1, q2), jnp.where(top8, r2, i2)))
                for k in range(2):
                    (re0, im0, u0), (re1, im1, u1) = out[k]
                    made.append((*dense(re0, re1, im0, im1), *dense_half(u0, u1)))
            for k, t in enumerate(made):
                at = j * owners + 4 * h + k
                for i in range(4):
                    reply_m[at, 8 * i : 8 * i + 8, :] = t[i]
                reply_t[at] = t[4]
            return 0

        lax.fori_loop(0, owners // 4, repack, 0, unroll=2)

    def reply(j, k):
        send_chunk(
            j, (k * size, k * size + size), reply_m, reply_t, back_m, back_t, turned_home if j == 0 else early_home, home_of, me_owner,
            s2m.at[j], s2t, r2m, r2t, sa,
        )

    def leave(j):
        wait_bytes(back_m, owners, j * owners, r2m.at[j])
        wait_bytes(back_t, owners, j * owners, r2t.at[j])

        def group(h, _):
            low = lane((8, 128)) < 64
            made = []
            for g in [2 * h, 2 * h + 1]:
                a, b = 2 * g, 2 * g + 1
                ta = [back_m[a, 8 * i : 8 * i + 8, :] for i in range(4)]
                tb = [back_m[b, 8 * i : 8 * i + 8, :] for i in range(4)]
                b0, b1, b3 = lroll(tb[0], 64), lroll(tb[1], 64), lroll(tb[3], 64)
                a1, a2 = lroll(ta[1], 64), lroll(ta[2], 64)
                re = (ta[0], jnp.where(low, ta[1], b0), jnp.where(low, b0, b1))
                im = (jnp.where(low, a1, a2), jnp.where(low, a2, tb[1]), tb[2])
                ra, rb = tail_rows(back_t[a]), tail_rows(back_t[b])
                u = (ta[3], jnp.where(low, ra, b3), jnp.where(low, b3, lroll(rb, 64)))
                for i in range(3):
                    k = 3 * g + i
                    at = pl.ds(pl.multiple_of(k * 128, 128), 128)
                    co, si, co4, si4 = [factors[n, :, at] for n in range(4)]
                    v = co4 * u[i] + si4 * sroll(u[i])
                    made.append((k, co * re[i] + si * im[i], co * im[i] - si * re[i], v))
            for k, re, im, v in made:
                outv[pl.ds(2 * k, 8, stride=per_row), :] = re
                outv[pl.ds(2 * k + 1, 8, stride=per_row), :] = im
                outv[pl.ds(8 * per_row + 2 * k, 4, stride=per_row), :] = v[0:4]
                outv[pl.ds(8 * per_row + 2 * k + 1, 4, stride=per_row), :] = v[4:8]
            return 0

        part = groups // CHUNKS // 2
        lax.fori_loop(j * part, (j + 1) * part, group, 0, unroll=2)
        width = per_row // CHUNKS

        def store(r, _):
            at = pl.ds(pl.multiple_of(r * per_row + j * width, 8), width)
            pltpu.make_async_copy(outv.at[at], out_h.at[at], out_sems.at[j]).start()
            return 0

        lax.fori_loop(0, ROWS, store, 0)

    advance(0)
    receive(0)
    advance(1)
    receive(1)
    finish(0)
    for k in ORDER:
        gate(2, k)
        reply(0, k)
    receive(2)
    finish(1)
    for k in range(GATES):
        reply(1, k)
    finish(2)
    for k in range(GATES):
        reply(2, k)
    for j in range(CHUNKS):
        leave(j)

    @pl.when(at_home)
    def _():
        to_other.wait_send()

    wait_sent(got_w, 0, s1w)
    for j in range(CHUNKS):
        wait_sent(sent_t, j * owners, s1t.at[j])

        @pl.when(has_up)
        def _(j=j):
            pltpu.make_async_copy(work.at[j], work.at[j], su.at[j]).wait()

        @pl.when(has_down)
        def _(j=j):
            pltpu.make_async_copy(work.at[j], work.at[j], sd.at[j]).wait()

    for j in range(CHUNKS):
        wait_sent(reply_m, j * owners, s2m.at[j])
        wait_sent(reply_t, j * owners, s2t.at[j])
        whole = pl.ds(0, ROWS * per_row // CHUNKS)
        pltpu.make_async_copy(outv.at[whole], out_h.at[whole], out_sems.at[j]).wait()


def body(wave_in, potential, absorb_radial, absorb_bond, coriolis_weight, ladder, angle_step, bond_step, radial_step):
    rows, columns = wave_in.shape[2:]
    blocks = columns // 128
    groups = blocks // 3
    bonds = 4 * groups
    nz = lax.axis_size("sa") // 4
    owners = 4 * nz
    top = lax.axis_size("ka") - 1
    count = radial_step.shape[1]
    hbm = pl.BlockSpec(memory_space=pl.ANY)
    wave = wave_in.reshape(2, rows, blocks, 128).transpose(1, 2, 0, 3).reshape(rows * blocks * 2, 128)
    messages = CHUNKS * owners
    dma, many = pltpu.SemaphoreType.DMA, pltpu.SemaphoreType.DMA((CHUNKS,))
    small = VMEM((256, 256), bf16)
    out = pl.pallas_call(
        functools.partial(step_kernel, groups, nz, top),
        out_shape=jax.ShapeDtypeStruct((rows * blocks * 2, 128), f32),
        in_specs=[hbm] * 9,
        out_specs=hbm,
        scratch_shapes=[
            VMEM((rows * blocks * 2, 128), f32),
            VMEM((rows, columns), f32),
            VMEM((1, rows), f32),
            VMEM((1, bonds), f32),
            VMEM((1, rows), f32),
            VMEM((1, 2, ANGLES, ANGLES), f32),
            VMEM((ANGLES, ANGLES), f32),
            VMEM((2, bonds, bonds), f32),
            VMEM((2, count, count), f32),
            VMEM((rows * (blocks + 1), 128), f32),
            VMEM((121 * groups, 128), f32),
            VMEM((CHUNKS, 4 * bonds // CHUNKS, 2 * bonds), bf16),
            VMEM((rows // 2, 2 * bonds, 256), f32),
            VMEM((rows // 2, 2 * bonds, 256), bf16),
            VMEM((rows // 2, 2 * bonds, 256), bf16),
            VMEM((3, groups, 128), f32),
            VMEM((4, 8, columns), f32),
            VMEM((messages, 32, 128), f32),
            VMEM((messages, 4, 128), f32),
            VMEM((messages, 32, 128), f32),
            VMEM((messages, 4, 128), f32),
            VMEM((owners, 1, 128), f32),
            VMEM((1, 128), f32),
            VMEM((count, 128), f32),
            VMEM((CHUNKS, 2, count, 256), f32),
            VMEM((CHUNKS, 2, count, 256), f32),
            VMEM((CHUNKS, 2, count, 256), f32),
            VMEM((messages, 32, 128), f32),
            VMEM((messages, 4, 128), f32),
            VMEM((messages, 32, 128), f32),
            VMEM((messages, 4, 128), f32),
            VMEM((rows * blocks * 2, 128), f32),
            small, small, small, small, small, small,
            VMEM((2 * count, 2 * count), bf16),
            VMEM((2 * count, 2 * count), bf16),
            VMEM((2 * count, 256), f32),
            VMEM((1, 2, ANGLES, ANGLES), f32),
            pltpu.SemaphoreType.DMA((8,)), pltpu.SemaphoreType.DMA((rows // 2,)), many, dma, dma,
            pltpu.SemaphoreType.DMA((CHUNKS, GATES)), many, dma, many, many, dma,
            many, many, many, many,
            many, many, many, many,
        ],
        compiler_params=pltpu.CompilerParams(collective_id=0, has_side_effects=True, vmem_limit_bytes=58 << 20),
        name="step",
    )(
        wave, potential, absorb_radial.reshape(1, -1), absorb_bond.reshape(1, -1), coriolis_weight.reshape(1, -1),
        angle_step, ladder, bond_step, radial_step,
    )
    return out.reshape(rows, blocks, 2, 128).transpose(2, 0, 1, 3).reshape(1, 2, rows, columns)


def solution(mesh):
    return jax.shard_map(
        body,
        mesh=mesh,
        in_specs=(
            P("ka", None, "sa", None),
            P("sa", None),
            P("sa"),
            P(),
            P("sa"),
            P(),
            P("ka", None, None, None),
            P(),
            P(),
        ),
        out_specs=P("ka", None, "sa", None),
        check_vma=False,
    )
```
